128 devices in a mesh: grp: 4 (over z), seq: 32 (over x, y, core).
Axes of the slice: x: 4, y: 4, z: 4, core: 2. Of those that a mesh axis runs over, the one named last changes fastest.
Arguments:
- projected: bfloat16 [32768, 3072], P(('grp', 'seq')), may hold values from -6 to 6
- conv_weight: float32 [4, 3072], replicated, may hold values from -3 to 3
- beta: float32 [8, 32768], P(None, ('grp', 'seq')), may hold values from 0 to 0.1, as said below
- gain: float32 [128], replicated, may hold values from 0.5 to 1.5
Outputs:
- normed: bfloat16 [32768, 1024], P(('grp', 'seq'))
The draws below stay inside these ranges and needn't reach their ends.
Inputs may be any that keep to these rules, and one draw needn't show every extreme that they name: `beta`: each head has its own rate, varying over tokens and devices, with a few stretches at the largest value.
All inputs are finite; a program needn't handle non-finite values.
Results may differ from the reference program's by a relative error of at most 0.001.
Values may be sent and summed in bfloat16 or wider, within the bound.
No kernel may reach another device: no remote copies, remote signals or barrier semaphores. Data moves between devices by JAX's collectives and lax.ppermute only.
A program may use at most 320 MiB of HBM per device.

```python
import math
import jax
import jax.numpy as jnp
from jax import lax

H = 8
DK = 128
KCONV = 4
SPAN = 128
TOK_DEV = 256
TOKENS = 32768


def draw_beta(key, part):
    key = jax.random.fold_in(key, 11)
    random_subkeys = jax.random.split(key, 4)
    bottom, top = (math.log(0.0001), math.log(0.1))
    base = jnp.exp(jax.random.uniform(random_subkeys[0], (H, 1), jnp.float32, bottom, top))
    blocks = jax.random.uniform(random_subkeys[1], (H, TOKENS // TOK_DEV, 1), jnp.float32, 0.5, 1.0)
    blocks = jnp.broadcast_to(blocks, (H, TOKENS // TOK_DEV, TOK_DEV)).reshape(H, TOKENS)
    rough = jax.random.uniform(random_subkeys[2], (H, TOKENS), jnp.float32, 0.5, 1.0)
    beta_rates = base * blocks * rough
    starts = jax.random.randint(random_subkeys[3], (H, 4), 0, TOKENS)
    position = jnp.arange(TOKENS)
    intra_block_pass = (position[None, None, :] >= starts[:, :, None]) & (position[None, None, :] < starts[:, :, None] + 256)
    segment_sweep = jnp.any(intra_block_pass, axis=1)
    beta_rates = jnp.where(segment_sweep, jnp.float32(0.1), jnp.minimum(beta_rates, jnp.float32(0.1)))
    return beta_rates.astype(jnp.float32)


def steps_of(own_key, extent, pieces, least, high):
    def one(dim, shards_of):
        draws = jax.random.uniform(jax.random.fold_in(jax.random.fold_in(own_key, 6), dim), (shards_of,), jnp.float32, least / len(pieces), high / len(pieces))
        return jnp.repeat(jnp.exp(draws), extent[dim] // shards_of).reshape((-1,) + (1,) * (len(extent) - dim - 1))

    loudness = one(*pieces[0])
    for cut in pieces[1:]:
        loudness = loudness * one(*cut)
    return loudness


def scatter_about(own_key, shape, scale, most, cuts=(), held_as=jnp.bfloat16):
    values = jax.random.normal(own_key, shape, jnp.float32) * scale
    if len(cuts) > 0:
        values = steps_of(own_key, shape, cuts, -0.22, 0.18) * values
    return jnp.clip(values, min=-most, max=most).astype(held_as)


def setup_inputs(seed: int = 0) -> dict:
    splits = jax.random.split(jax.random.key(seed), 5)
    projected = scatter_about(splits[0], (TOKENS, 3 * H * DK), 1.0, 6.0, ((0, 128),))
    conv_weight = scatter_about(splits[1], (KCONV, 3 * H * DK), KCONV ** -0.5, 3.0, (), jnp.float32)
    beta = draw_beta(jax.random.fold_in(splits[4], 71), 0)
    gain = jnp.clip(jax.random.uniform(splits[3], (DK,), jnp.float32, 0.5, 1.5), 0.5, 1.5)
    return {"projected": projected, "conv_weight": conv_weight, "beta": beta, "gain": gain}


def contract(form, left, right):
    return jnp.einsum(form, left, right, precision=lax.Precision.HIGHEST)

def conv_silu(extended, conv_weight, rows):
    mixed = jnp.zeros((rows, extended.shape[1]), jnp.float32)
    for offset in range(KCONV):
        mixed = mixed + conv_weight[offset] * extended[offset:offset + rows]
    return jax.nn.silu(mixed)

def unit_rows(values):
    return values / jnp.sqrt(lax.optimization_barrier(jnp.sum(values * values, -1, keepdims=True)) + 1e-06)

def split_heads(mixed):
    rows = mixed.shape[0]
    parts = mixed.reshape(rows // SPAN, SPAN, 3, H, DK).transpose(2, 3, 0, 1, 4)
    return (unit_rows(parts[0]), unit_rows(parts[1]), parts[2])

def unit_lower_inverse(inner, size):
    negated = -inner
    power = negated
    result = jnp.eye(size, dtype=jnp.float32) + negated
    reach = 2
    while reach < size:
        power = contract('...ij,...jk->...ik', power, power)
        result = result + contract('...ij,...jk->...ik', result, power)
        reach = reach * 2
    return result

def span_terms(queries, keys, values, beta_rates):
    size = keys.shape[-2]
    strict = jnp.tril(jnp.ones((size, size), jnp.float32), -1)
    inclusive = jnp.tril(jnp.ones((size, size), jnp.float32), 0)
    inner = contract('...id,...jd->...ij', beta_rates * keys, keys) * strict
    inverse = unit_lower_inverse(inner, size)
    right_side = jnp.concatenate([beta_rates * keys, beta_rates * values], -1)
    solved = contract('...ij,...jd->...id', inverse, right_side)
    width = keys.shape[-1]
    scores = contract('...id,...jd->...ij', queries, keys) * inclusive
    return (solved[..., :width], solved[..., width:], scores)

def finish(outputs, gain):
    rows = outputs.shape[0]
    spread = jnp.sqrt(lax.optimization_barrier(jnp.mean(outputs * outputs, -1, keepdims=True)) + 1e-06)
    return (outputs / spread * gain).astype(jnp.bfloat16).reshape(rows, H * DK)

def reference(projected, conv_weight, beta, gain):
    rows = projected.shape[0]
    extended = jnp.concatenate([jnp.zeros((KCONV - 1, projected.shape[1]), jnp.float32), projected.astype(jnp.float32)], 0)
    mixed = conv_silu(extended, conv_weight, rows)
    queries, keys, values = split_heads(mixed)
    beta_rates = beta.reshape(H, rows // SPAN, SPAN, 1)
    blocks = tuple((item.transpose(1, 0, 2, 3) for item in (queries, keys, values, beta_rates)))

    def advance(state, block):
        block_queries, block_keys, block_values, block_rates = block
        w_keys, u_values, scores = span_terms(block_queries, block_keys, block_values, block_rates)
        fresh = u_values - contract('hcd,hde->hce', w_keys, state)
        output = contract('hcd,hde->hce', block_queries, state) + contract('hcj,hjd->hcd', scores, fresh)
        state = state + contract('hcd,hce->hde', block_keys, fresh)
        return (state, output)
    start_state = jnp.zeros((H, DK, DK), jnp.float32)
    _, outputs = lax.scan(advance, start_state, blocks)
    outputs = outputs.transpose(0, 2, 1, 3).reshape(rows, H, DK)
    return finish(outputs, gain)
```

```python
import functools

import jax
import jax.numpy as jnp
from jax import lax
from jax.experimental import pallas as pl
from jax.experimental.pallas import tpu as pltpu
from jax.sharding import Mesh
from jax.sharding import PartitionSpec as P

H = 8
DK = 128
KCONV = 4
HALF = H // 2
ROWS = 256
F32, BF16 = jnp.float32, jnp.bfloat16
ALL = ("z", "x", "y", "core")
VMEM_BYTES = 48 * 1024 * 1024


def split(a):
    high = a.astype(BF16)
    return high, (a - high.astype(F32)).astype(BF16)


def dot(a, b):
    return jnp.dot(a, b, preferred_element_type=F32)


def mm(a, b):
    a_high, a_low = split(a)
    b_high, b_low = split(b)
    wide = jnp.concatenate([b_high, b_low], 1)
    r = dot(jnp.concatenate([a_high, a_low], 1), jnp.concatenate([wide, wide], 0))
    n = b.shape[1]
    return r[:, :n] + r[:, n:]


def mmw(a, b):
    a_high, a_low = split(a)
    b_high, b_low = split(b)
    if a.shape[1] == 128:
        r = dot(jnp.concatenate([a_high, a_low], 1), jnp.concatenate([b_high, b_high], 0))
        return r + dot(a_high, b_low)
    return (dot(a_high, b_high) + dot(a_low, b_high)) + dot(a_high, b_low)


def places(size):
    r = lax.broadcasted_iota(jnp.int32, (size, size), 0)
    c = lax.broadcasted_iota(jnp.int32, (size, size), 1)
    return r, c


def unit_lower_inverses(inners):
    r, c = places(128)
    eye = (r == c).astype(F32)
    n1 = [jnp.where((r // 16) == (c // 16), -a, 0.0) for a in inners]
    n2 = [mm(n, n) for n in n1]
    n4 = [mm(n, n) for n in n2]
    inv = [(eye + a) + mm(eye + a, b) for a, b in zip(n1, n2)]
    n8 = [mm(n, n) for n in n4]
    inv = [d + mm(d, n) for d, n in zip(inv, n4)]
    inv = [d + mm(d, n) for d, n in zip(inv, n8)]
    for size in (16, 32, 64):
        below = ((r // (2 * size)) == (c // (2 * size))) & ((r // size) != (c // size))
        part = [mm(jnp.where(below, a, 0.0), d) for a, d in zip(inners, inv)]
        inv = [d - mm(d, m) for d, m in zip(inv, part)]
    return inv


def unit(values):
    return values * lax.rsqrt(jnp.sum(values * values, -1, keepdims=True) + 1e-06)


def local_kernel(
    at, xq, xk, xv, rq, rk, rv, wq, wk, wv, beta, trans_out, q_out, o_out, scratch
):
    heads = range(HALF)

    def mixed(p, x, rim, w, h):
        cols = slice(h * DK, (h + 1) * DK)
        scratch[p, h, 5:8, :] = rim[:, cols].astype(F32)
        scratch[p, h, 8 : 8 + ROWS, :] = x[:, cols].astype(F32)
        acc = w[0:1, cols] * scratch[p, h, 5 : 5 + ROWS, :]
        for j in range(1, KCONV):
            acc = acc + w[j : j + 1, cols] * scratch[p, h, 5 + j : 5 + j + ROWS, :]
        return acc / (1.0 + jnp.exp(-acc))

    keys = [unit(mixed(1, xk, rk, wk, h)) for h in heads]
    queries = [unit(mixed(0, xq, rq, wq, h)) for h in heads]
    values = [mixed(2, xv, rv, wv, h) for h in heads]
    rates = [beta[h].reshape(1, ROWS) for h in heads]
    keys_t = [k.T for k in keys]
    r, c = places(ROWS)
    grams = [mmw(jnp.concatenate([q, k], 0), kt) for q, k, kt in zip(queries, keys, keys_t)]
    scores = [jnp.where(r >= c, g[:ROWS] * b, 0.0) for g, b in zip(grams, rates)]
    inner = [jnp.where(r > c, g[ROWS:] * b, 0.0) for g, b in zip(grams, rates)]
    right = [jnp.concatenate([k, v], 1) for k, v in zip(keys, values)]
    inv = unit_lower_inverses([a[:128, :128] for a in inner] + [a[128:, 128:] for a in inner])
    first = [mmw(d, x[:128]) for d, x in zip(inv[:HALF], right)]
    rest = [x[128:] - mmw(a[128:, :128], y) for x, a, y in zip(right, inner, first)]
    second = [mmw(d, z) for d, z in zip(inv[HALF:], rest)]
    solved = [jnp.concatenate([a, b], 0) for a, b in zip(first, second)]
    trans = [mmw(kt * b, y) for kt, b, y in zip(keys_t, rates, solved)]
    r, c = places(DK)
    for h in heads:
        trans_out[h, :, :DK] = jnp.where(r == c, 1.0, 0.0) - trans[h][:, :DK]
        trans_out[h, :, DK:] = trans[h][:, DK:]
    out = [mmw(s, y) for s, y in zip(scores, solved)]
    for h in heads:
        q_out[h] = queries[h] - out[h][:, :DK]
        o_out[h] = out[h][:, DK:]


def compose(later, earlier):
    m = mmw(later[:, :DK], earlier)
    return jnp.concatenate([m[:, :DK], m[:, DK:] + later[:, DK:]], 1)


def enter(trans, state):
    return mm(trans[:, :DK], state) + trans[:, DK:]


def pair_kernel(at, kept, came, *outs):
    y, core = at[2], at[3]
    for d in range(4):
        j = lax.rem(y + d, 4)
        own, other = kept[j], came[j]
        outs[d][...] = compose(
            jnp.where(core == 0, other, own), jnp.where(core == 0, own, other)
        )


def ring_prefix(place, blocks, held):
    for d, block in enumerate(blocks):
        held[lax.rem(place + 4 - d, 4)] = block[...]


def y_kernel(at, b0, b1, b2, b3, total, prefixes, held):
    ring_prefix(at[2], (b0, b1, b2, b3), held)
    one = held[0]
    two = compose(held[1], one)
    upper = compose(held[3], held[2])
    prefixes[0] = one
    prefixes[1] = two
    prefixes[2] = compose(held[2], two)
    total[...] = compose(upper, two)


def x_kernel(at, b0, b1, b2, b3, total, prefix, held):
    x = at[1]
    ring_prefix(x, (b0, b1, b2, b3), held)
    one = held[0]
    two = compose(held[1], one)
    upper = compose(held[3], held[2])
    three = compose(held[2], two)
    r, c = places(DK)
    none = jnp.concatenate([jnp.where(r == c, 1.0, 0.0), jnp.zeros((DK, DK), F32)], 1)
    low = jnp.where(x == 0, none, one)
    high = jnp.where(x == 2, two, three)
    prefix[...] = jnp.where(x < 2, low, high)
    total[...] = compose(upper, two)


def z_kernel(at, b1, b2, b3, x_prefix, y_prefixes, s0, s1, s2, s3, states):
    y, z = at[2], at[0]
    state = jnp.where(z >= 3, b3[:, DK:], 0.0)
    state = enter(b2[...], state)
    state = enter(b1[...], state)
    state = enter(x_prefix[...], state)
    states[0] = state
    for i in range(3):
        states[i + 1] = enter(y_prefixes[i], state)
    for d, out in enumerate((s0, s1, s2, s3)):
        out[...] = states[lax.rem(y + d, 4)]


def core_kernel(at, kept, came, s0, s1, s2, s3, stays, goes):
    y, core = at[2], at[3]
    for d, state in enumerate((s0, s1, s2, s3)):
        j = lax.rem(y + 4 - d, 4)
        first = state[...]
        second = enter(jnp.where(core == 0, kept[j], came[j]), first)
        stays[j] = jnp.where(core == 0, first, second)
        goes[j] = jnp.where(core == 0, second, first)


def final_kernel(at, q_own, o_own, s_own, q_far, o_far, s_far, gain, out):
    core = at[3]

    def finish(q, o, s, base):
        for h in range(HALF):
            r = mm(q[h], s[h]) + o[h]
            r = r * lax.rsqrt(jnp.mean(r * r, -1, keepdims=True) + 1e-06) * gain[...]
            cols = pl.ds(pl.multiple_of((base + h) * DK, DK), DK)
            out[:, cols] = r.astype(BF16)

    finish(q_own, o_own, s_own, core * HALF)
    finish(q_far, o_far, s_far, (1 - core) * HALF)


def whole(shape):
    return pl.BlockSpec(shape, lambda *_: (0,) * len(shape))


def call(kernel, at, args, outs, scratch=(), flops=0):
    args = list(args)
    return pl.pallas_call(
        kernel,
        grid_spec=pltpu.PrefetchScalarGridSpec(
            num_scalar_prefetch=1,
            grid=(1,),
            in_specs=[whole(a.shape) for a in args],
            out_specs=[whole(o.shape) for o in outs],
            scratch_shapes=list(scratch),
        ),
        out_shape=list(outs),
        cost_estimate=pl.CostEstimate(flops=flops, bytes_accessed=2**20, transcendentals=0),
        compiler_params=pltpu.CompilerParams(vmem_limit_bytes=VMEM_BYTES),
    )(at, *args)


def local_call(at, projected, rim, weight, beta, other):
    def group(a):
        return 1 - a[3] if other else a[3]

    def cols(rows, part):
        return pl.BlockSpec((rows, HALF * DK), lambda i, a: (0, 2 * part + group(a)))

    return pl.pallas_call(
        local_kernel,
        grid_spec=pltpu.PrefetchScalarGridSpec(
            num_scalar_prefetch=1,
            grid=(1,),
            in_specs=[cols(ROWS, p) for p in range(3)]
            + [cols(KCONV - 1, p) for p in range(3)]
            + [cols(KCONV, p) for p in range(3)]
            + [pl.BlockSpec((HALF, 1, ROWS), lambda i, a: (group(a), 0, 0))],
            out_specs=[
                whole((HALF, DK, 2 * DK)),
                whole((HALF, ROWS, DK)),
                whole((HALF, ROWS, DK)),
            ],
            scratch_shapes=[pltpu.VMEM((3, HALF, ROWS + 8, DK), F32)],
        ),
        out_shape=[
            jax.ShapeDtypeStruct((HALF, DK, 2 * DK), F32),
            jax.ShapeDtypeStruct((HALF, ROWS, DK), F32),
            jax.ShapeDtypeStruct((HALF, ROWS, DK), F32),
        ],
        cost_estimate=pl.CostEstimate(
            flops=4 * 10**9, bytes_accessed=3 * 2**20, transcendentals=10**6
        ),
        compiler_params=pltpu.CompilerParams(vmem_limit_bytes=VMEM_BYTES),
    )(at, *[projected] * 3, *[rim] * 3, *[weight] * 3, beta)


def swap(block):
    return lax.ppermute(block, "core", [(0, 1), (1, 0)])


def shift(block, axis, distance, wrap=True):
    n = lax.axis_size(axis)
    route = [(i, (i + distance) % n) for i in range(n) if wrap or i + distance < n]
    return lax.ppermute(block, axis, route)


def shards(projected, weight, beta, gain):
    at = jnp.stack([lax.axis_index(a) for a in ALL]).astype(jnp.int32)
    count = lax.axis_size(ALL)
    rim = lax.ppermute(
        projected[ROWS - (KCONV - 1) :], ALL, [(i, i + 1) for i in range(count - 1)]
    )
    beta = beta.reshape(H, 1, ROWS)
    sent, q_far, o_far = local_call(at, projected, rim, weight, beta, True)
    came = swap(sent)
    kept, q_own, o_own = local_call(at, projected, rim, weight, beta, False)

    block = jax.ShapeDtypeStruct((DK, 2 * DK), F32)
    state = jax.ShapeDtypeStruct((DK, DK), F32)
    three = jax.ShapeDtypeStruct((3, DK, 2 * DK), F32)
    held = pltpu.VMEM((4, DK, 2 * DK), F32)
    chip = call(pair_kernel, at, (kept, came), [block] * 4)
    ring = [chip[0]] + [shift(chip[d], "y", d) for d in (1, 2, 3)]
    total, y_prefixes = call(y_kernel, at, ring, [block, three], [held])
    ring = [total] + [shift(total, "x", d) for d in (1, 2, 3)]
    total, x_prefix = call(x_kernel, at, ring, [block, block], [held])
    line = [shift(total, "z", d, False) for d in (1, 2, 3)]
    states = call(
        z_kernel,
        at,
        (*line, x_prefix, y_prefixes),
        [state] * 4,
        [pltpu.VMEM((4, DK, DK), F32)],
    )
    states = [states[0]] + [shift(states[d], "y", d) for d in (1, 2, 3)]
    four = jax.ShapeDtypeStruct((HALF, DK, DK), F32)
    s_own, goes = call(core_kernel, at, (kept, came, *states), [four] * 2)
    s_far = swap(goes)
    (out,) = call(
        final_kernel,
        at,
        (q_own, o_own, s_own, q_far, o_far, s_far, gain.reshape(1, DK)),
        [jax.ShapeDtypeStruct((ROWS, H * DK), BF16)],
    )
    return out


def solution(mesh):
    grid = Mesh(mesh.devices.reshape(4, 4, 4, 2), ALL)
    placed = (P(ALL, None), P(), P(None, ALL), P())
    return jax.shard_map(
        shards, mesh=grid, in_specs=placed, out_specs=P(ALL, None), check_vma=False
    )
```

```python
import functools

import jax
import jax.numpy as jnp
from jax import lax
from jax.experimental import pallas as pl
from jax.experimental.pallas import tpu as pltpu
from jax.sharding import Mesh
from jax.sharding import PartitionSpec as P

H = 8
DK = 128
KCONV = 4
HALF = H // 2
ROWS = 256
F32, BF16 = jnp.float32, jnp.bfloat16
ALL = ("z", "x", "y", "core")
VMEM_BYTES = 48 * 1024 * 1024
MIX_BYTES = 103 * 512 * 1024


def split(a):
    high = a.astype(BF16)
    return high, (a - high.astype(F32)).astype(BF16)


def dot(a, b):
    return jnp.dot(a, b, preferred_element_type=F32)


def mm(a, b):
    a_high, a_low = split(a)
    b_high, b_low = split(b)
    wide = jnp.concatenate([b_high, b_low], 1)
    r = dot(jnp.concatenate([a_high, a_low], 1), jnp.concatenate([wide, wide], 0))
    n = b.shape[1]
    return r[:, :n] + r[:, n:]


def mmw(a, b):
    a_high, a_low = split(a)
    b_high, b_low = split(b)
    if a.shape[1] == 128:
        r = dot(jnp.concatenate([a_high, a_low], 1), jnp.concatenate([b_high, b_high], 0))
        return r + dot(a_high, b_low)
    return (dot(a_high, b_high) + dot(a_low, b_high)) + dot(a_high, b_low)


def places(size):
    r = lax.broadcasted_iota(jnp.int32, (size, size), 0)
    c = lax.broadcasted_iota(jnp.int32, (size, size), 1)
    return r, c


def mm64(a, b):
    high = a.astype(BF16)
    wide = high.astype(F32)
    both = (wide + pltpu.roll(a - wide, 64, 1)).astype(BF16)
    b_high, b_low = split(b)
    return dot(
        jnp.concatenate([both, high], 1), jnp.concatenate([b_high, b_high, b_low, b_low], 0)
    )


def alternate(a, size):
    return jnp.concatenate([a[i : i + size] for i in range(size, 128, 2 * size)], 0)


def between(upper, lower, size):
    parts = []
    for i in range(0, 64, size):
        parts += [upper[i : i + size], lower[i : i + size]]
    return jnp.concatenate(parts, 0)


def half_inverses(inners):
    r, c = places(128)
    lane = lax.broadcasted_iota(jnp.int32, (16, 128), 1)
    row = lax.broadcasted_iota(jnp.int32, (16, 128), 0)
    folded = []
    for a in inners:
        f = jnp.zeros((16, 128), F32)
        for b in range(8):
            f = jnp.where(lane // 16 == b, a[16 * b : 16 * b + 16], f)
        folded.append(f)
    inv = [jnp.where(row == lane % 16, 1.0, 0.0)] * len(inners)
    for j in range(15):
        spread = (lane // 16) * 16 + j
        inv = [
            x
            - jnp.where(
                row > j, jnp.take_along_axis(f, spread, axis=1, mode="promise_in_bounds"), 0.0
            )
            * x[j : j + 1]
            for f, x in zip(folded, inv)
        ]
    inv = [jnp.where(r // 16 == c // 16, jnp.concatenate([x] * 8, 0), 0.0) for x in inv]
    zero = jnp.zeros((64, 128), F32)
    for size in (16, 32):
        below = ((r // (2 * size)) == (c // (2 * size))) & ((r // size) != (c // size))
        part = [mm(alternate(jnp.where(below, a, 0.0), size), d) for a, d in zip(inners, inv)]
        low = [
            alternate(d, size) - mm(alternate(d, size), between(zero, m, size))
            for d, m in zip(inv, part)
        ]
        inv = [
            between(
                jnp.concatenate([d[i : i + size] for i in range(0, 128, 2 * size)], 0), x, size
            )
            for d, x in zip(inv, low)
        ]
    return inv


def unit(values):
    return values * lax.rsqrt(jnp.sum(values * values, -1, keepdims=True) + 1e-06)


def silu(a):
    return a / (1.0 + jnp.exp(-a))


def taps(w, rows, scratch, count):
    acc = w[0:1, :] * scratch[5 : 5 + count, :]
    for j in range(1, KCONV):
        acc = acc + w[j : j + 1, :] * scratch[5 + j : 5 + j + count, :]
    return silu(acc)


def columns(h):
    return slice(h * DK, (h + 1) * DK)


HEADS = range(HALF)


def mix_kernel(at, x_all, w_all, keys_out, values_out, x_out, w_out, x_in, scratch, sems):
    copies = []
    for g in range(2):
        for p in range(2):
            begin = pl.multiple_of(
                ((p + 1) * H + half_of(at, g == 0) * HALF) * DK, HALF * DK
            )
            one = pltpu.make_async_copy(
                w_all.at[:, pl.ds(begin, HALF * DK)], w_out.at[g, p], sems.at[0, g, p]
            )
            one.start()
            two = pltpu.make_async_copy(
                x_all.at[:, pl.ds(begin, HALF * DK)], x_in.at[g, p], sems.at[1, g, p]
            )
            two.start()
            copies.append((one, two))
    for g in range(2):
        for p in range(2):
            for copy in copies[2 * g + p]:
                copy.wait()
            for h in HEADS:
                held = scratch.at[g, p, h]
                held[0:8, :] = jnp.zeros((8, DK), F32)
                held[8 : 8 + ROWS, :] = x_in[g, p, :, columns(h)].astype(F32)
                x_out[g, p, :, columns(h)] = held[8:16, :]
                m = taps(w_out[g, p, :, columns(h)], ROWS, held, ROWS)
                if p == 0:
                    keys_out[g * HALF + h] = unit(m)
                else:
                    values_out[g * HALF + h] = m


def first_rows(rim, x, w, scratch, h):
    scratch[5:8, :] = rim[:, columns(h)].astype(F32)
    scratch[8:16, :] = x[:, columns(h)]
    return taps(w[:, columns(h)], 8, scratch, 8)


def local_kernel(
    at, keys_in, values_in, x, w, rk, rv, beta, trans_out, keys_out, solved_out, scratch, *, other
):
    half = half_of(at, other)
    keys = [
        jnp.concatenate(
            [unit(first_rows(rk, x.at[0, 0], w.at[0, 0], scratch.at[0, h], h)), keys_in[h, 8:, :]], 0
        )
        for h in HEADS
    ]
    values = [
        jnp.concatenate(
            [first_rows(rv, x.at[0, 1], w.at[0, 1], scratch.at[1, h], h), values_in[h, 8:, :]], 0
        )
        for h in HEADS
    ]
    keys_t = [k.T * beta[pl.ds(half * HALF + h, 1), :] for h, k in zip(HEADS, keys)]
    r, c = places(128)
    strict = r > c
    top = [jnp.where(strict, mm(k[:128], kt[:, :128]), 0.0) for k, kt in zip(keys, keys_t)]
    below = [mmw(k[128:], kt) for k, kt in zip(keys, keys_t)]
    inner = top + [jnp.where(strict, a[:, 128:], 0.0) for a in below]
    right = [jnp.concatenate([k, v], 1) for k, v in zip(keys, values)]
    inv = half_inverses(inner)
    left = lax.broadcasted_iota(jnp.int32, (64, 128), 1) < 64

    def solve(diagonal, strictly, x):
        first = [mm64(d[:64], b[:64]) for d, b in zip(diagonal, x)]
        rest = [
            b[64:] - mm64(jnp.where(left, a[64:], 0.0), y) for b, a, y in zip(x, strictly, first)
        ]
        second = [mm64(d[64:], z) for d, z in zip(diagonal, rest)]
        return [jnp.concatenate([a, b], 0) for a, b in zip(first, second)]

    first = solve(inv[:HALF], inner[:HALF], [x[:128] for x in right])
    rest = [x[128:] - mmw(a[:, :128], y) for x, a, y in zip(right, below, first)]
    second = solve(inv[HALF:], inner[HALF:], rest)
    solved = [jnp.concatenate([a, b], 0) for a, b in zip(first, second)]
    trans = [mmw(kt, y) for kt, y in zip(keys_t, solved)]
    for h in HEADS:
        trans_out[h, :, :DK] = jnp.where(r == c, 1.0, 0.0) - trans[h][:, :DK]
        trans_out[h, :, DK:] = trans[h][:, DK:]
        keys_out[h] = keys_t[h]
        solved_out[h] = solved[h]


def output_kernel(at, xq, rq, wq, keys_t, solved, q_out, o_out, token, scratch):
    token[...] = jnp.zeros_like(token)
    queries = []
    for h in HEADS:
        held = scratch.at[h]
        held[5:8, :] = rq[:, columns(h)].astype(F32)
        held[8 : 8 + ROWS, :] = xq[:, columns(h)].astype(F32)
        queries.append(unit(taps(wq[:, columns(h)], ROWS, held, ROWS)))
    r, c = places(ROWS)
    scores = [jnp.where(r >= c, mmw(q, keys_t[h]), 0.0) for h, q in zip(HEADS, queries)]
    out = [mmw(s, solved[h]) for h, s in zip(HEADS, scores)]
    for h in HEADS:
        q_out[h] = queries[h] - out[h][:, :DK]
        o_out[h] = out[h][:, DK:]


def compose(later, earlier):
    m = mmw(later[:, :DK], earlier)
    return jnp.concatenate([m[:, :DK], m[:, DK:] + later[:, DK:]], 1)


def enter(trans, state):
    return mm(trans[:, :DK], state) + trans[:, DK:]


def ordered(own_first, own, other):
    return jnp.where(own_first, other, own), jnp.where(own_first, own, other)


def chip_kernel(at, kept, came, *outs):
    for d in range(4):
        j = lax.rem(at[2] + d, 4)
        outs[d][...] = compose(*ordered(at[3] == 0, kept[j], came[j]))


def y_kernel(at, b0, b1, b2, b3, total, prefixes, held):
    y = at[2]
    for d, block in enumerate((b0, b1, b2, b3)):
        held[lax.rem(y + 4 - d, 4)] = block[...]
    one = held[0]
    two = compose(held[1], one)
    upper = compose(held[3], held[2])
    prefixes[0] = one
    prefixes[1] = two
    prefixes[2] = compose(held[2], two)
    total[...] = compose(upper, two)


def x_kernel(at, b0, b1, b2, b3, total, prefix, held):
    x = at[1]
    for d, block in enumerate((b0, b1, b2, b3)):
        held[lax.rem(x + 4 - d, 4)] = block[...]
    one = held[0]
    two = compose(held[1], one)
    upper = compose(held[3], held[2])
    three = compose(held[2], two)
    r, c = places(DK)
    none = jnp.concatenate([jnp.where(r == c, 1.0, 0.0), jnp.zeros((DK, DK), F32)], 1)
    prefix[...] = jnp.where(
        x < 2, jnp.where(x == 0, none, one), jnp.where(x == 2, two, three)
    )
    total[...] = compose(upper, two)


def z_kernel(at, b1, b2, b3, x_prefix, y_prefixes, s0, s1, s2, s3, states):
    y, z = at[2], at[0]
    state = jnp.where(z >= 3, b3[:, DK:], 0.0)
    state = jnp.where(z >= 2, enter(b2[...], state), 0.0)
    state = jnp.where(z >= 1, enter(b1[...], state), 0.0)
    state = enter(x_prefix[...], state)
    states[0] = state
    for i in range(3):
        states[i + 1] = enter(y_prefixes[i], state)
    for d, out in enumerate((s0, s1, s2, s3)):
        out[...] = states[lax.rem(y + d, 4)]


def core_kernel(at, kept, came, s0, s1, s2, s3, stays, goes):
    y, low = at[2], at[3] == 0
    for d, state in enumerate((s0, s1, s2, s3)):
        j = lax.rem(y + 4 - d, 4)
        first = state[...]
        second = enter(jnp.where(low, kept[j], came[j]), first)
        stays[j] = jnp.where(low, first, second)
        goes[j] = jnp.where(low, second, first)


def finished(q, o, s, gain, h):
    r = mm(q[h], s[h]) + o[h]
    return (r * lax.rsqrt(jnp.mean(r * r, -1, keepdims=True) + 1e-06) * gain[...]).astype(BF16)


def final_own_kernel(at, q, o, s, gain, out):
    for h in HEADS:
        out[:, columns(h)] = finished(q, o, s, gain, h)


def final_kernel(at, q, o, s, gain, own, out):
    half = HALF * DK
    out[:, pl.ds(pl.multiple_of(at[3] * half, half), half)] = own[...]
    for h in HEADS:
        begin = pl.multiple_of((1 - at[3]) * half + h * DK, DK)
        out[:, pl.ds(begin, DK)] = finished(q, o, s, gain, h)


def whole(shape):
    return pl.BlockSpec(shape, lambda *_: (0,) * len(shape))


ANYWHERE = pl.BlockSpec(memory_space=pl.ANY)


def call(
    kernel, at, args, in_specs, outs, out_specs, scratch=(), after=(), vmem=VMEM_BYTES
):
    args, after = list(args), list(after)

    def body(at_ref, *refs):
        kernel(at_ref, *refs[: len(args)], *refs[len(args) + len(after) :])

    return pl.pallas_call(
        body,
        grid_spec=pltpu.PrefetchScalarGridSpec(
            num_scalar_prefetch=1,
            grid=(1,),
            in_specs=list(in_specs) + [ANYWHERE] * len(after),
            out_specs=list(out_specs),
            scratch_shapes=list(scratch),
        ),
        out_shape=list(outs),
        cost_estimate=pl.CostEstimate(flops=10**6, bytes_accessed=2**10, transcendentals=0),
        compiler_params=pltpu.CompilerParams(vmem_limit_bytes=vmem),
    )(at, *args, *after)


def step(kernel, at, args, outs, scratch=(), after=()):
    return call(
        kernel,
        at,
        args,
        [whole(a.shape) for a in args],
        outs,
        [whole(o.shape) for o in outs],
        scratch,
        after,
    )


def half_of(a, other):
    return 1 - a[3] if other else a[3]


def cols(rows, part, other):
    return pl.BlockSpec((rows, HALF * DK), lambda i, a: (0, 2 * part + half_of(a, other)))


def shaped(*shape):
    return jax.ShapeDtypeStruct(shape, F32)


def mix_call(at, projected, weight):
    hbm = pl.BlockSpec(memory_space=pltpu.HBM)
    outs = [shaped(H, ROWS, DK)] * 2 + [shaped(2, 2, 8, HALF * DK), shaped(2, 2, KCONV, HALF * DK)]
    return call(
        mix_kernel,
        at,
        [projected, weight],
        [hbm, hbm],
        outs,
        [whole(o.shape) for o in outs],
        [
            pltpu.VMEM((2, 2, ROWS, HALF * DK), BF16),
            pltpu.VMEM((2, 2, HALF, ROWS + 8, DK), F32),
            pltpu.SemaphoreType.DMA((2, 2, 2)),
        ],
        vmem=MIX_BYTES,
    )


def local_call(at, mixes, rim, beta, other):
    keys, values, x, w = mixes
    place = int(not other)
    block = pl.BlockSpec((HALF, ROWS, DK), lambda i, a: (place, 0, 0))
    specs = [block, block]
    specs += [pl.BlockSpec((1, *a.shape[1:]), lambda i, a: (place, 0, 0, 0)) for a in (x, w)]
    specs += [cols(KCONV - 1, 1, other), cols(KCONV - 1, 2, other), whole(beta.shape)]
    outs = [shaped(HALF, DK, 2 * DK), shaped(HALF, DK, ROWS), shaped(HALF, ROWS, 2 * DK)]
    return call(
        functools.partial(local_kernel, other=other),
        at,
        [keys, values, x, w, rim, rim, beta],
        specs,
        outs,
        [whole(o.shape) for o in outs],
        [pltpu.VMEM((2, HALF, 16, DK), F32)],
    )


def output_call(at, projected, rim, weight, keys_t, solved, other):
    specs = [cols(rows, 0, other) for rows in (ROWS, KCONV - 1, KCONV)]
    specs += [whole(keys_t.shape), whole(solved.shape)]
    outs = [shaped(HALF, ROWS, DK), shaped(HALF, ROWS, DK), shaped(8, DK)]
    return call(
        output_kernel,
        at,
        [projected, rim, weight, keys_t, solved],
        specs,
        outs,
        [whole(o.shape) for o in outs],
        [pltpu.VMEM((HALF, ROWS + 8, DK), F32)],
    )


def swap(block):
    return lax.ppermute(block, "core", [(0, 1), (1, 0)])


def shift(block, axis, distance):
    n = lax.axis_size(axis)
    return lax.ppermute(block, axis, [(i, (i + distance) % n) for i in range(n)])


def shards(projected, weight, beta, gain):
    at = jnp.stack([lax.axis_index(a) for a in ALL]).astype(jnp.int32)
    count = lax.axis_size(ALL)
    rim = lax.ppermute(
        projected[ROWS - (KCONV - 1) :], ALL, [(i, i + 1) for i in range(count - 1)]
    )
    gain = gain.reshape(1, DK)
    one, state = shaped(DK, 2 * DK), shaped(DK, DK)

    mixes = mix_call(at, projected, weight)
    sent, keys_far, solved_far = local_call(at, mixes, rim, beta, True)
    came = swap(sent)
    kept, keys_own, solved_own = local_call(at, mixes, rim, beta, False)
    chip = step(chip_kernel, at, (kept, came), [one] * 4)

    held = pltpu.VMEM((4, DK, 2 * DK), F32)
    ring = [chip[0]] + [shift(chip[d], "y", d) for d in (1, 2, 3)]
    q_far, o_far, far_done = output_call(at, projected, rim, weight, keys_far, solved_far, True)
    q_own, o_own, own_done = output_call(at, projected, rim, weight, keys_own, solved_own, False)
    trans, y_prefixes = step(
        y_kernel, at, ring, [one, shaped(3, DK, 2 * DK)], [held], (far_done, own_done)
    )
    ring = [trans] + [shift(trans, "x", d) for d in (1, 2, 3)]
    trans, x_prefix = step(x_kernel, at, ring, [one, one], [held])
    before = [shift(trans, "z", d) for d in (1, 2, 3)]

    states = step(
        z_kernel,
        at,
        (*before, x_prefix, y_prefixes),
        [state] * 4,
        [pltpu.VMEM((4, DK, DK), F32)],
    )
    states = [states[0]] + [shift(states[d], "y", d) for d in (1, 2, 3)]
    s_own, goes = step(core_kernel, at, (kept, came, *states), [shaped(HALF, DK, DK)] * 2)
    s_far = swap(goes)
    half = jax.ShapeDtypeStruct((ROWS, HALF * DK), BF16)
    (own,) = step(final_own_kernel, at, (q_own, o_own, s_own, gain), [half])
    out = jax.ShapeDtypeStruct((ROWS, H * DK), BF16)
    return step(final_kernel, at, (q_far, o_far, s_far, gain, own), [out])[0]


def solution(mesh):
    grid = Mesh(mesh.devices.reshape(4, 4, 4, 2), ALL)
    placed = (P(ALL, None), P(), P(None, ALL), P())
    return jax.shard_map(
        shards, mesh=grid, in_specs=placed, out_specs=P(ALL, None), check_vma=False
    )
```

```python
import functools

import jax
import jax.numpy as jnp
from jax import lax
from jax.experimental import pallas as pl
from jax.experimental.pallas import tpu as pltpu
from jax.sharding import Mesh
from jax.sharding import PartitionSpec as P

H = 8
DK = 128
KCONV = 4
HALF = H // 2
ROWS = 256
F32, BF16 = jnp.float32, jnp.bfloat16
ALL = ("z", "x", "y", "core")
VMEM_BYTES = 48 * 1024 * 1024
MIX_BYTES = 103 * 512 * 1024


def split(a):
    high = a.astype(BF16)
    return high, (a - high.astype(F32)).astype(BF16)


def dot(a, b):
    return jnp.dot(a, b, preferred_element_type=F32)


def mm(a, b):
    a_high, a_low = split(a)
    b_high, b_low = split(b)
    wide = jnp.concatenate([b_high, b_low], 1)
    r = dot(jnp.concatenate([a_high, a_low], 1), jnp.concatenate([wide, wide], 0))
    n = b.shape[1]
    return r[:, :n] + r[:, n:]


def mmw(a, b):
    a_high, a_low = split(a)
    b_high, b_low = split(b)
    if a.shape[1] == 128:
        r = dot(jnp.concatenate([a_high, a_low], 1), jnp.concatenate([b_high, b_high], 0))
        return r + dot(a_high, b_low)
    return (dot(a_high, b_high) + dot(a_low, b_high)) + dot(a_high, b_low)


def places(size):
    r = lax.broadcasted_iota(jnp.int32, (size, size), 0)
    c = lax.broadcasted_iota(jnp.int32, (size, size), 1)
    return r, c


def alternate(a, size):
    return jnp.concatenate([a[i : i + size] for i in range(size, 128, 2 * size)], 0)


def between(upper, lower, size):
    parts = []
    for i in range(0, 64, size):
        parts += [upper[i : i + size], lower[i : i + size]]
    return jnp.concatenate(parts, 0)


def unit_lower_inverses(inners):
    r, c = places(128)
    lane = lax.broadcasted_iota(jnp.int32, (16, 128), 1)
    row = lax.broadcasted_iota(jnp.int32, (16, 128), 0)
    folded = []
    for a in inners:
        f = jnp.zeros((16, 128), F32)
        for b in range(8):
            f = jnp.where(lane // 16 == b, a[16 * b : 16 * b + 16], f)
        folded.append(f)
    inv = [jnp.where(row == lane % 16, 1.0, 0.0)] * len(inners)
    for j in range(15):
        spread = (lane // 16) * 16 + j
        inv = [
            x
            - jnp.where(
                row > j, jnp.take_along_axis(f, spread, axis=1, mode="promise_in_bounds"), 0.0
            )
            * x[j : j + 1]
            for f, x in zip(folded, inv)
        ]
    inv = [jnp.where(r // 16 == c // 16, jnp.concatenate([x] * 8, 0), 0.0) for x in inv]
    zero = jnp.zeros((64, 128), F32)
    for size in (16, 32, 64):
        below = ((r // (2 * size)) == (c // (2 * size))) & ((r // size) != (c // size))
        part = [mm(alternate(jnp.where(below, a, 0.0), size), d) for a, d in zip(inners, inv)]
        low = [
            alternate(d, size) - mm(alternate(d, size), between(zero, m, size))
            for d, m in zip(inv, part)
        ]
        inv = [
            between(
                jnp.concatenate([d[i : i + size] for i in range(0, 128, 2 * size)], 0), x, size
            )
            for d, x in zip(inv, low)
        ]
    return inv


def unit(values):
    return values * lax.rsqrt(jnp.sum(values * values, -1, keepdims=True) + 1e-06)


def silu(a):
    return a / (1.0 + jnp.exp(-a))


def taps(w, rows, scratch, count):
    acc = w[0:1, :] * scratch[5 : 5 + count, :]
    for j in range(1, KCONV):
        acc = acc + w[j : j + 1, :] * scratch[5 + j : 5 + j + count, :]
    return silu(acc)


def columns(h):
    return slice(h * DK, (h + 1) * DK)


def half_of(at, other):
    return 1 - at[3] if other else at[3]


def head_columns(part, half, h):
    return pl.ds(pl.multiple_of((part * H + half * HALF + h) * DK, DK), DK)


HEADS = range(HALF)


def mix_kernel(x_in, w_in, keys_out, values_out, x_out, scratch):
    for p in range(2):
        for h in HEADS:
            held = scratch.at[p, h]
            held[0:8, :] = jnp.zeros((8, DK), F32)
            held[8 : 8 + ROWS, :] = x_in[p, :, columns(h)].astype(F32)
            x_out[p, :, columns(h)] = held[8:16, :]
            m = taps(w_in[p, :, columns(h)], ROWS, held, ROWS)
            if p == 0:
                keys_out[h] = unit(m)
            else:
                values_out[h] = m


def mix_own_kernel(at, x_in, w_in, *refs):
    mix_kernel(x_in, w_in, *refs)


def mix_far_kernel(at, x_all, w_all, *refs):
    keys_out, values_out, x_out, w_far, w_own, x_own, x_far, scratch, sems = refs
    copies = []
    for i, (other, x_to, w_to) in enumerate(((True, x_far, w_far), (False, x_own, w_own))):
        for p in range(2):
            begin = pl.multiple_of(
                ((p + 1) * H + half_of(at, other) * HALF) * DK, HALF * DK
            )
            cols = pl.ds(begin, HALF * DK)
            k = 4 * i + 2 * p
            copies.append(pltpu.make_async_copy(w_all.at[:, cols], w_to.at[p], sems.at[k]))
            copies.append(pltpu.make_async_copy(x_all.at[:, cols], x_to.at[p], sems.at[k + 1]))
    for copy in copies:
        copy.start()
    for copy in copies[:4]:
        copy.wait()
    mix_kernel(x_far, w_far, keys_out, values_out, x_out, scratch)
    for copy in copies[4:]:
        copy.wait()


def rim_of(at, rim, cols):
    first = at[0] + at[1] + at[2] + at[3] == 0
    return jnp.where(first, 0.0, rim[:, cols].astype(F32))


def first_rows(rim, x, w, scratch):
    scratch[5:8, :] = rim
    scratch[8:16, :] = x
    return taps(w, 8, scratch, 8)


def local_kernel(
    at, keys_in, values_in, x, w, rim, beta, trans_out, keys_out, solved_out, scratch, *, other
):
    half = half_of(at, other)

    def with_rim(p, h, rest):
        first = first_rows(
            rim_of(at, rim, head_columns(p + 1, half, h)),
            x[p, :, columns(h)],
            w[p, :, columns(h)],
            scratch.at[p, h],
        )
        return jnp.concatenate([unit(first) if p == 0 else first, rest[h, 8:, :]], 0)

    keys = [with_rim(0, h, keys_in) for h in HEADS]
    values = [with_rim(1, h, values_in) for h in HEADS]
    keys_t = [k.T * beta[pl.ds(half * HALF + h, 1), :] for h, k in zip(HEADS, keys)]
    r, c = places(128)
    strict = r > c
    top = [jnp.where(strict, mm(k[:128], kt[:, :128]), 0.0) for k, kt in zip(keys, keys_t)]
    below = [mmw(k[128:], kt) for k, kt in zip(keys, keys_t)]
    inner = top + [jnp.where(strict, a[:, 128:], 0.0) for a in below]
    right = [jnp.concatenate([k, v], 1) for k, v in zip(keys, values)]
    inv = unit_lower_inverses(inner)
    first = [mmw(d, x[:128]) for d, x in zip(inv[:HALF], right)]
    rest = [x[128:] - mmw(a[:, :128], y) for x, a, y in zip(right, below, first)]
    second = [mmw(d, z) for d, z in zip(inv[HALF:], rest)]
    solved = [jnp.concatenate([a, b], 0) for a, b in zip(first, second)]
    trans = [mmw(kt, y) for kt, y in zip(keys_t, solved)]
    for h in HEADS:
        trans_out[h, :, :DK] = jnp.where(r == c, 1.0, 0.0) - trans[h][:, :DK]
        trans_out[h, :, DK:] = trans[h][:, DK:]
        keys_out[h] = keys_t[h]
        solved_out[h] = solved[h]


def output_kernel(at, x, rim, w, keys_t, solved, q_out, o_out, token, scratch, *, other):
    token[...] = jnp.zeros_like(token)
    half = half_of(at, other)
    queries = []
    for h in HEADS:
        held, cols = scratch.at[h], head_columns(0, half, h)
        held[5:8, :] = rim_of(at, rim, cols)
        held[8 : 8 + ROWS, :] = x[:, cols].astype(F32)
        queries.append(unit(taps(w[:, cols], ROWS, held, ROWS)))
    r, c = places(ROWS)
    scores = [jnp.where(r >= c, mmw(q, keys_t[h]), 0.0) for h, q in zip(HEADS, queries)]
    out = [mmw(s, solved[h]) for h, s in zip(HEADS, scores)]
    for h in HEADS:
        q_out[h] = queries[h] - out[h][:, :DK]
        o_out[h] = out[h][:, DK:]


def compose(later, earlier):
    m = mmw(later[:, :DK], earlier)
    return jnp.concatenate([m[:, :DK], m[:, DK:] + later[:, DK:]], 1)


def enter(trans, state):
    return mm(trans[:, :DK], state) + trans[:, DK:]


def ordered(own_first, own, other):
    return jnp.where(own_first, other, own), jnp.where(own_first, own, other)


def chip_kernel(at, kept, came, *outs):
    for d in range(4):
        j = lax.rem(at[2] + d, 4)
        outs[d][...] = compose(*ordered(at[3] == 0, kept[j], came[j]))


def y_kernel(at, b0, b2, b1, b3, total, prefixes, held):
    y = at[2]
    for d, block in enumerate((b0, b1, b2, b3)):
        held[lax.rem(y + 4 - d, 4)] = block[...]
    one = held[0]
    two = compose(held[1], one)
    upper = compose(held[3], held[2])
    prefixes[0] = one
    prefixes[1] = two
    prefixes[2] = compose(held[2], two)
    total[...] = compose(upper, two)


def x_kernel(at, b0, b1, b3, b2, total, prefix, held):
    x = at[1]
    for d, block in enumerate((b0, b1, b2, b3)):
        held[lax.rem(x + 4 - d, 4)] = block[...]
    one = held[0]
    two = compose(held[1], one)
    upper = compose(held[3], held[2])
    three = compose(held[2], two)
    r, c = places(DK)
    none = jnp.concatenate([jnp.where(r == c, 1.0, 0.0), jnp.zeros((DK, DK), F32)], 1)
    prefix[...] = jnp.where(
        x < 2, jnp.where(x == 0, none, one), jnp.where(x == 2, two, three)
    )
    total[...] = compose(upper, two)


def z_kernel(at, b1, b3, b2, x_prefix, y_prefixes, s0, s1, s2, s3, states):
    y, z = at[2], at[0]
    state = jnp.where(z >= 3, b3[:, DK:], 0.0)
    state = jnp.where(z >= 2, enter(b2[...], state), 0.0)
    state = jnp.where(z >= 1, enter(b1[...], state), 0.0)
    state = enter(x_prefix[...], state)
    states[0] = state
    for i in range(3):
        states[i + 1] = enter(y_prefixes[i], state)
    for d, out in enumerate((s0, s1, s2, s3)):
        out[...] = states[lax.rem(y + d, 4)]


def core_kernel(at, kept, came, s0, s2, s1, s3, stays, goes):
    y, low = at[2], at[3] == 0
    for d, state in enumerate((s0, s1, s2, s3)):
        j = lax.rem(y + 4 - d, 4)
        first = state[...]
        second = enter(jnp.where(low, kept[j], came[j]), first)
        stays[j] = jnp.where(low, first, second)
        goes[j] = jnp.where(low, second, first)


def finished(q, o, s, gain, h):
    r = mm(q[h], s[h]) + o[h]
    return (r * lax.rsqrt(jnp.mean(r * r, -1, keepdims=True) + 1e-06) * gain[...]).astype(BF16)


def final_own_kernel(at, q, o, s, gain, out):
    for h in HEADS:
        out[:, columns(h)] = finished(q, o, s, gain, h)


def final_kernel(at, q, o, s, gain, own, out):
    for h in HEADS:
        out[:, head_columns(0, at[3], h)] = own[:, columns(h)]
        out[:, head_columns(0, 1 - at[3], h)] = finished(q, o, s, gain, h)


class Place:
    def __getitem__(self, i):
        return lax.axis_index(ALL[i])


def step(kernel, args, outs, scratch=(), after=(), vmem=VMEM_BYTES, hbm=()):
    args, after, hbm = list(args), list(after), list(hbm)

    def body(*refs):
        kernel(Place(), *refs[: len(args) + len(hbm)], *refs[len(args) + len(hbm) + len(after) :])

    anywhere = pl.BlockSpec(memory_space=pl.ANY)
    return pl.pallas_call(
        body,
        in_specs=[pl.BlockSpec()] * len(args) + [anywhere] * (len(hbm) + len(after)),
        out_shape=list(outs),
        scratch_shapes=list(scratch),
        cost_estimate=pl.CostEstimate(flops=10**6, bytes_accessed=2**10, transcendentals=0),
        compiler_params=pltpu.CompilerParams(vmem_limit_bytes=vmem),
    )(*args, *hbm, *after)


def shaped(*shape):
    return jax.ShapeDtypeStruct(shape, F32)


def mix_calls(projected, weight):
    mixed = [shaped(HALF, ROWS, DK)] * 2 + [shaped(2, 8, HALF * DK)]
    w, x = shaped(2, KCONV, HALF * DK), jax.ShapeDtypeStruct((2, ROWS, HALF * DK), BF16)
    room = pltpu.VMEM((2, HALF, ROWS + 8, DK), F32)
    *far, w_own, x_own = step(
        mix_far_kernel,
        (),
        [*mixed, w, w, x],
        [
            pltpu.VMEM(x.shape, BF16),
            room,
            pltpu.SemaphoreType.DMA((8,)),
        ],
        vmem=MIX_BYTES,
        hbm=(projected, weight),
    )
    own = step(mix_own_kernel, (x_own, w_own), mixed, [room])
    return far, [*own, w_own]


def local_call(mixes, rim, beta, other, after=()):
    outs = [shaped(HALF, DK, 2 * DK), shaped(HALF, DK, ROWS), shaped(HALF, ROWS, 2 * DK)]
    return step(
        functools.partial(local_kernel, other=other),
        (*mixes, rim, beta),
        outs,
        [pltpu.VMEM((2, HALF, 16, DK), F32)],
        after,
    )


def output_call(projected, rim, weight, keys_t, solved, other):
    outs = [shaped(HALF, ROWS, DK), shaped(HALF, ROWS, DK), shaped(8, DK)]
    return step(
        functools.partial(output_kernel, other=other),
        (projected, rim, weight, keys_t, solved),
        outs,
        [pltpu.VMEM((HALF, ROWS + 8, DK), F32)],
    )


def swap(block):
    return lax.ppermute(block, "core", [(0, 1), (1, 0)])


def shift(block, axis, distance):
    n = lax.axis_size(axis)
    return lax.ppermute(block, axis, [(i, (i + distance) % n) for i in range(n)])


def ring_of(blocks, axis):
    return [shift(block, axis, d + 1) for d, block in enumerate(blocks)]


def shards(projected, weight, beta, gain):
    gain = gain.reshape(1, DK)
    one, state = shaped(DK, 2 * DK), shaped(DK, DK)

    last = projected[ROWS - (KCONV - 1) :]
    count = lax.axis_size(ALL)
    rim = lax.ppermute(last, ALL, [(i, (i + 1) % count) for i in range(count)])
    mixes_far, mixes_own = mix_calls(projected, weight)
    sent, keys_far, solved_far = local_call(mixes_far, rim, beta, True, mixes_own[2:3])
    came = swap(sent)
    kept, keys_own, solved_own = local_call(mixes_own, rim, beta, False)
    chip = step(chip_kernel, (kept, came), [one] * 4)

    held = pltpu.VMEM((4, DK, 2 * DK), F32)
    b1, b2, b3 = ring_of(chip[1:], "y")
    q_far, o_far, far_done = output_call(projected, rim, weight, keys_far, solved_far, True)
    q_own, o_own, own_done = output_call(projected, rim, weight, keys_own, solved_own, False)
    trans, y_prefixes = step(
        y_kernel,
        (chip[0], b2, b1, b3),
        [one, shaped(3, DK, 2 * DK)],
        [held],
        (far_done, own_done),
    )
    b1, b2, b3 = ring_of([trans] * 3, "x")
    trans, x_prefix = step(x_kernel, (trans, b1, b3, b2), [one, one], [held])
    b1, b2, b3 = ring_of([trans] * 3, "z")

    states = step(
        z_kernel,
        (b1, b3, b2, x_prefix, y_prefixes),
        [state] * 4,
        [pltpu.VMEM((4, DK, DK), F32)],
    )
    s1, s2, s3 = ring_of(states[1:], "y")
    s_own, goes = step(core_kernel, (kept, came, states[0], s2, s1, s3), [shaped(HALF, DK, DK)] * 2)
    s_far = swap(goes)
    half = jax.ShapeDtypeStruct((ROWS, HALF * DK), BF16)
    (own,) = step(final_own_kernel, (q_own, o_own, s_own, gain), [half])
    out = jax.ShapeDtypeStruct((ROWS, H * DK), BF16)
    return step(final_kernel, (q_far, o_far, s_far, gain, own), [out])[0]


def solution(mesh):
    grid = Mesh(mesh.devices.reshape(4, 4, 4, 2), ALL)
    placed = (P(ALL, None), P(), P(None, ALL), P())
    return jax.shard_map(
        shards, mesh=grid, in_specs=placed, out_specs=P(ALL, None), check_vma=False
    )
```

```python
import functools

import jax
import jax.numpy as jnp
from jax import lax
from jax.experimental import pallas as pl
from jax.experimental.pallas import tpu as pltpu
from jax.sharding import Mesh
from jax.sharding import PartitionSpec as P

H = 8
DK = 128
KCONV = 4
HALF = H // 2
ROWS = 256
F32, BF16 = jnp.float32, jnp.bfloat16
ALL = ("z", "x", "y", "core")
VMEM_BYTES = 48 * 1024 * 1024
FETCH_BYTES = 52 * 1024 * 1024
FETCH_FLOPS = 10**9


def split(a):
    high = a.astype(BF16)
    return high, (a - high.astype(F32)).astype(BF16)


def dot(a, b):
    return jnp.dot(a, b, preferred_element_type=F32)


def mm(a, b):
    a_high, a_low = split(a)
    b_high, b_low = split(b)
    wide = jnp.concatenate([b_high, b_low], 1)
    r = dot(jnp.concatenate([a_high, a_low], 1), jnp.concatenate([wide, wide], 0))
    n = b.shape[1]
    return r[:, :n] + r[:, n:]


def mmw(a, b):
    a_high, a_low = split(a)
    b_high, b_low = split(b)
    if a.shape[1] == 128:
        r = dot(jnp.concatenate([a_high, a_low], 1), jnp.concatenate([b_high, b_high], 0))
        return r + dot(a_high, b_low)
    return (dot(a_high, b_high) + dot(a_low, b_high)) + dot(a_high, b_low)


def places(size):
    r = lax.broadcasted_iota(jnp.int32, (size, size), 0)
    c = lax.broadcasted_iota(jnp.int32, (size, size), 1)
    return r, c


def alternate(a, size):
    return jnp.concatenate([a[i : i + size] for i in range(size, 128, 2 * size)], 0)


def between(upper, lower, size):
    parts = []
    for i in range(0, 64, size):
        parts += [upper[i : i + size], lower[i : i + size]]
    return jnp.concatenate(parts, 0)


def unit_lower_inverses(inners):
    r, c = places(128)
    lane = lax.broadcasted_iota(jnp.int32, (16, 128), 1)
    row = lax.broadcasted_iota(jnp.int32, (16, 128), 0)
    folded = []
    for a in inners:
        f = jnp.zeros((16, 128), F32)
        for b in range(8):
            f = jnp.where(lane // 16 == b, a[16 * b : 16 * b + 16], f)
        folded.append(f)
    inv = [jnp.where(row == lane % 16, 1.0, 0.0)] * len(inners)
    for j in range(15):
        spread = (lane // 16) * 16 + j
        inv = [
            x
            - jnp.where(
                row > j, jnp.take_along_axis(f, spread, axis=1, mode="promise_in_bounds"), 0.0
            )
            * x[j : j + 1]
            for f, x in zip(folded, inv)
        ]
    inv = [jnp.where(r // 16 == c // 16, jnp.concatenate([x] * 8, 0), 0.0) for x in inv]
    zero = jnp.zeros((64, 128), F32)
    for size in (16, 32, 64):
        below = ((r // (2 * size)) == (c // (2 * size))) & ((r // size) != (c // size))
        part = [mm(alternate(jnp.where(below, a, 0.0), size), d) for a, d in zip(inners, inv)]
        low = [
            alternate(d, size) - mm(alternate(d, size), between(zero, m, size))
            for d, m in zip(inv, part)
        ]
        inv = [
            between(
                jnp.concatenate([d[i : i + size] for i in range(0, 128, 2 * size)], 0), x, size
            )
            for d, x in zip(inv, low)
        ]
    return inv


def unit(values):
    return values * lax.rsqrt(jnp.sum(values * values, -1, keepdims=True) + 1e-06)


def silu(a):
    return a / (1.0 + jnp.exp(-a))


def taps(w, rows, scratch, count):
    acc = w[0:1, :] * scratch[5 : 5 + count, :]
    for j in range(1, KCONV):
        acc = acc + w[j : j + 1, :] * scratch[5 + j : 5 + j + count, :]
    return silu(acc)


def columns(h):
    return slice(h * DK, (h + 1) * DK)


def half_of(at, other):
    return 1 - at[3] if other else at[3]


def head_columns(part, half, h):
    return pl.ds(pl.multiple_of((part * H + half * HALF + h) * DK, DK), DK)


HEADS = range(HALF)


def fetch_kernel(at, x_all, last_out, x_far, x_own, tail, sems):
    copies = [pltpu.make_async_copy(x_all.at[pl.ds(ROWS - 16, 16), :], tail, sems.at[4])]
    for g, to in enumerate((x_far, x_own)):
        for p in range(2):
            begin = ((p + 1) * H + half_of(at, g == 0) * HALF) * DK
            cols = pl.ds(pl.multiple_of(begin, HALF * DK), HALF * DK)
            copies.append(
                pltpu.make_async_copy(x_all.at[:, cols], to.at[p], sems.at[2 * g + p])
            )
    for copy in copies:
        copy.start()
    for copy in copies:
        copy.wait()
    last_out[...] = tail[...].astype(F32)[16 - (KCONV - 1) :].astype(BF16)


def mix_kernel(at, x, w, keys_out, values_out, x_out, scratch, *, other):
    half = half_of(at, other)
    for p in range(2):
        for h in HEADS:
            held = scratch.at[p, h]
            held[0:8, :] = jnp.zeros((8, DK), F32)
            held[8 : 8 + ROWS, :] = x[p, :, columns(h)].astype(F32)
            x_out[p, :, columns(h)] = held[8:16, :]
            m = taps(w[:, head_columns(p + 1, half, h)], ROWS, held, ROWS)
            if p == 0:
                keys_out[h] = unit(m)
            else:
                values_out[h] = m


def rim_of(at, rim, cols):
    first = at[0] + at[1] + at[2] + at[3] == 0
    return jnp.where(first, 0.0, rim[:, cols].astype(F32))


def first_rows(rim, x, w, scratch):
    scratch[5:8, :] = rim
    scratch[8:16, :] = x
    return taps(w, 8, scratch, 8)


def local_kernel(
    at, keys_in, values_in, x, w, rim, beta, trans_out, keys_out, solved_out, scratch, *, other
):
    half = half_of(at, other)

    def with_rim(p, h, rest):
        first = first_rows(
            rim_of(at, rim, head_columns(p + 1, half, h)),
            x[p, :, columns(h)],
            w[:, head_columns(p + 1, half, h)],
            scratch.at[p, h],
        )
        return jnp.concatenate([unit(first) if p == 0 else first, rest[h, 8:, :]], 0)

    keys = [with_rim(0, h, keys_in) for h in HEADS]
    values = [with_rim(1, h, values_in) for h in HEADS]
    keys_t = [k.T * beta[pl.ds(half * HALF + h, 1), :] for h, k in zip(HEADS, keys)]
    r, c = places(128)
    strict = r > c
    top = [jnp.where(strict, mm(k[:128], kt[:, :128]), 0.0) for k, kt in zip(keys, keys_t)]
    below = [mmw(k[128:], kt) for k, kt in zip(keys, keys_t)]
    inner = top + [jnp.where(strict, a[:, 128:], 0.0) for a in below]
    right = [jnp.concatenate([k, v], 1) for k, v in zip(keys, values)]
    inv = unit_lower_inverses(inner)
    first = [mmw(d, x[:128]) for d, x in zip(inv[:HALF], right)]
    rest = [x[128:] - mmw(a[:, :128], y) for x, a, y in zip(right, below, first)]
    second = [mmw(d, z) for d, z in zip(inv[HALF:], rest)]
    solved = [jnp.concatenate([a, b], 0) for a, b in zip(first, second)]
    trans = [mmw(kt, y) for kt, y in zip(keys_t, solved)]
    for h in HEADS:
        trans_out[h, :, :DK] = jnp.where(r == c, 1.0, 0.0) - trans[h][:, :DK]
        trans_out[h, :, DK:] = trans[h][:, DK:]
        keys_out[h] = keys_t[h]
        solved_out[h] = solved[h]


def output_kernel(at, x, rim, w, keys_t, solved, q_out, o_out, token, scratch, *, other):
    token[...] = jnp.zeros_like(token)
    half = half_of(at, other)
    queries = []
    for h in HEADS:
        held, cols = scratch.at[h], head_columns(0, half, h)
        held[5:8, :] = rim_of(at, rim, cols)
        held[8 : 8 + ROWS, :] = x[:, cols].astype(F32)
        queries.append(unit(taps(w[:, cols], ROWS, held, ROWS)))
    r, c = places(ROWS)
    scores = [jnp.where(r >= c, mmw(q, keys_t[h]), 0.0) for h, q in zip(HEADS, queries)]
    out = [mmw(s, solved[h]) for h, s in zip(HEADS, scores)]
    for h in HEADS:
        q_out[h] = queries[h] - out[h][:, :DK]
        o_out[h] = out[h][:, DK:]


def compose(later, earlier):
    m = mmw(later[:, :DK], earlier)
    return jnp.concatenate([m[:, :DK], m[:, DK:] + later[:, DK:]], 1)


def enter(trans, state):
    return mm(trans[:, :DK], state) + trans[:, DK:]


def ordered(own_first, own, other):
    return jnp.where(own_first, other, own), jnp.where(own_first, own, other)


def chip_kernel(at, kept, came, *outs):
    for d in range(4):
        j = lax.rem(at[2] + d, 4)
        outs[d][...] = compose(*ordered(at[3] == 0, kept[j], came[j]))


def y_kernel(at, b0, b2, b1, b3, total, prefixes, held):
    y = at[2]
    for d, block in enumerate((b0, b1, b2, b3)):
        held[lax.rem(y + 4 - d, 4)] = block[...]
    one = held[0]
    two = compose(held[1], one)
    upper = compose(held[3], held[2])
    prefixes[0] = one
    prefixes[1] = two
    prefixes[2] = compose(held[2], two)
    total[...] = compose(upper, two)


def x_kernel(at, b0, b1, b3, b2, total, prefix, held):
    x = at[1]
    for d, block in enumerate((b0, b1, b2, b3)):
        held[lax.rem(x + 4 - d, 4)] = block[...]
    one = held[0]
    two = compose(held[1], one)
    upper = compose(held[3], held[2])
    three = compose(held[2], two)
    r, c = places(DK)
    none = jnp.concatenate([jnp.where(r == c, 1.0, 0.0), jnp.zeros((DK, DK), F32)], 1)
    prefix[...] = jnp.where(
        x < 2, jnp.where(x == 0, none, one), jnp.where(x == 2, two, three)
    )
    total[...] = compose(upper, two)


def z1_kernel(at, own, got, second):
    later, earlier = ordered(at[0] % 2 == 0, own[...], got[...])
    second[...] = enter(later, earlier[:, DK:])


def z2_kernel(at, got_z, got_second, x_prefix, y_prefixes, s0, s1, s2, s3, states):
    z, y = at[0], at[2]
    state = jnp.where(
        z < 2,
        jnp.where(z == 0, 0.0, got_z[:, DK:]),
        jnp.where(z == 2, got_second[...], enter(got_z[...], got_second[...])),
    )
    state = enter(x_prefix[...], state)
    states[0] = state
    for i in range(3):
        states[i + 1] = enter(y_prefixes[i], state)
    for d, out in enumerate((s0, s1, s2, s3)):
        out[...] = states[lax.rem(y + d, 4)]


def core_kernel(at, kept, came, s0, s2, s1, s3, stays, goes):
    y, low = at[2], at[3] == 0
    for d, state in enumerate((s0, s1, s2, s3)):
        j = lax.rem(y + 4 - d, 4)
        first = state[...]
        second = enter(jnp.where(low, kept[j], came[j]), first)
        stays[j] = jnp.where(low, first, second)
        goes[j] = jnp.where(low, second, first)


def finished(q, o, s, gain, h):
    r = mm(q[h], s[h]) + o[h]
    return (r * lax.rsqrt(jnp.mean(r * r, -1, keepdims=True) + 1e-06) * gain[...]).astype(BF16)


def final_own_kernel(at, q, o, s, gain, out):
    for h in HEADS:
        out[:, columns(h)] = finished(q, o, s, gain, h)


def final_kernel(at, q, o, s, gain, own, out):
    for h in HEADS:
        out[:, head_columns(0, at[3], h)] = own[:, columns(h)]
        out[:, head_columns(0, 1 - at[3], h)] = finished(q, o, s, gain, h)


class Place:
    def __getitem__(self, i):
        return lax.axis_index(ALL[i])


def step(kernel, args, outs, scratch=(), after=(), vmem=VMEM_BYTES, hbm=(), flops=10**6):
    args, after, hbm = list(args), list(after), list(hbm)

    def body(*refs):
        kernel(Place(), *refs[: len(args) + len(hbm)], *refs[len(args) + len(hbm) + len(after) :])

    anywhere = pl.BlockSpec(memory_space=pl.ANY)
    return pl.pallas_call(
        body,
        in_specs=[pl.BlockSpec()] * len(args) + [anywhere] * (len(hbm) + len(after)),
        out_shape=list(outs),
        scratch_shapes=list(scratch),
        cost_estimate=pl.CostEstimate(flops=flops, bytes_accessed=2**10, transcendentals=0),
        compiler_params=pltpu.CompilerParams(vmem_limit_bytes=vmem),
    )(*args, *hbm, *after)


def shaped(*shape):
    return jax.ShapeDtypeStruct(shape, F32)


def fetch_call(projected):
    x = jax.ShapeDtypeStruct((2, ROWS, HALF * DK), BF16)
    return step(
        fetch_kernel,
        (),
        [jax.ShapeDtypeStruct((KCONV - 1, 3 * H * DK), BF16), x, x],
        [pltpu.VMEM((16, 3 * H * DK), BF16), pltpu.SemaphoreType.DMA((5,))],
        vmem=FETCH_BYTES,
        hbm=(projected,),
        flops=FETCH_FLOPS,
    )


def mix_call(x, weight, other):
    return step(
        functools.partial(mix_kernel, other=other),
        (x, weight),
        [shaped(HALF, ROWS, DK)] * 2 + [shaped(2, 8, HALF * DK)],
        [pltpu.VMEM((2, HALF, ROWS + 8, DK), F32)],
    )


def local_call(mixes, weight, rim, beta, other, after=()):
    outs = [shaped(HALF, DK, 2 * DK), shaped(HALF, DK, ROWS), shaped(HALF, ROWS, 2 * DK)]
    return step(
        functools.partial(local_kernel, other=other),
        (*mixes, weight, rim, beta),
        outs,
        [pltpu.VMEM((2, HALF, 16, DK), F32)],
        after,
    )


def output_call(projected, rim, weight, keys_t, solved, other):
    outs = [shaped(HALF, ROWS, DK), shaped(HALF, ROWS, DK), shaped(8, DK)]
    return step(
        functools.partial(output_kernel, other=other),
        (projected, rim, weight, keys_t, solved),
        outs,
        [pltpu.VMEM((HALF, ROWS + 8, DK), F32)],
    )


def exchange(block, axis, partner):
    return lax.ppermute(block, axis, [(i, partner(i)) for i in range(lax.axis_size(axis))])


def swap(block):
    return exchange(block, "core", lambda i: 1 - i)


def shift(block, axis, distance):
    n = lax.axis_size(axis)
    return lax.ppermute(block, axis, [(i, (i + distance) % n) for i in range(n)])


def ring_of(blocks, axis):
    return [shift(block, axis, d + 1) for d, block in enumerate(blocks)]


def shards(projected, weight, beta, gain):
    gain = gain.reshape(1, DK)
    one, state = shaped(DK, 2 * DK), shaped(DK, DK)

    last, x_far, x_own = fetch_call(projected)
    count = lax.axis_size(ALL)
    rim = lax.ppermute(last, ALL, [(i, (i + 1) % count) for i in range(count)])
    mixes_far = mix_call(x_far, weight, True)
    mixes_own = mix_call(x_own, weight, False)
    sent, keys_far, solved_far = local_call(
        mixes_far, weight, rim, beta, True, mixes_own[2:]
    )
    came = swap(sent)
    kept, keys_own, solved_own = local_call(mixes_own, weight, rim, beta, False)
    chip = step(chip_kernel, (kept, came), [one] * 4)

    held = pltpu.VMEM((4, DK, 2 * DK), F32)
    b1, b2, b3 = ring_of(chip[1:], "y")
    q_far, o_far, far_done = output_call(projected, rim, weight, keys_far, solved_far, True)
    q_own, o_own, own_done = output_call(projected, rim, weight, keys_own, solved_own, False)
    trans, y_prefixes = step(
        y_kernel,
        (chip[0], b2, b1, b3),
        [one, shaped(3, DK, 2 * DK)],
        [held],
        (far_done, own_done),
    )
    b1, b2, b3 = ring_of([trans] * 3, "x")
    trans, x_prefix = step(x_kernel, (trans, b1, b3, b2), [one, one], [held])
    got_z = exchange(trans, "z", lambda i: i ^ 1)
    (second,) = step(z1_kernel, (trans, got_z), [state])
    got_second = exchange(second, "z", lambda i: 3 - i)

    states = step(
        z2_kernel,
        (got_z, got_second, x_prefix, y_prefixes),
        [state] * 4,
        [pltpu.VMEM((4, DK, DK), F32)],
    )
    s1, s2, s3 = ring_of(states[1:], "y")
    s_own, goes = step(core_kernel, (kept, came, states[0], s2, s1, s3), [shaped(HALF, DK, DK)] * 2)
    s_far = swap(goes)
    half = jax.ShapeDtypeStruct((ROWS, HALF * DK), BF16)
    (own,) = step(final_own_kernel, (q_own, o_own, s_own, gain), [half])
    out = jax.ShapeDtypeStruct((ROWS, H * DK), BF16)
    return step(final_kernel, (q_far, o_far, s_far, gain, own), [out])[0]


def solution(mesh):
    grid = Mesh(mesh.devices.reshape(4, 4, 4, 2), ALL)
    placed = (P(ALL, None), P(), P(None, ALL), P())
    return jax.shard_map(
        shards, mesh=grid, in_specs=placed, out_specs=P(ALL, None), check_vma=False
    )
```

```python
import functools

import jax
import jax.numpy as jnp
from jax import lax
from jax.experimental import pallas as pl
from jax.experimental.pallas import tpu as pltpu
from jax.sharding import Mesh
from jax.sharding import PartitionSpec as P

H = 8
DK = 128
KCONV = 4
HALF = H // 2
ROWS = 256
F32, BF16 = jnp.float32, jnp.bfloat16
ALL = ("z", "x", "y", "core")
VMEM_BYTES = 48 * 1024 * 1024
FETCH_BYTES = 52 * 1024 * 1024
FETCH_FLOPS = 10**9


def split(a):
    high = a.astype(BF16)
    return high, (a - high.astype(F32)).astype(BF16)


def dot(a, b):
    return jnp.dot(a, b, preferred_element_type=F32)


def mm(a, b):
    a_high, a_low = split(a)
    b_high, b_low = split(b)
    wide = jnp.concatenate([b_high, b_low], 1)
    r = dot(jnp.concatenate([a_high, a_low], 1), jnp.concatenate([wide, wide], 0))
    n = b.shape[1]
    return r[:, :n] + r[:, n:]


def mmw(a, b):
    a_high, a_low = split(a)
    b_high, b_low = split(b)
    if a.shape[1] == 128:
        r = dot(jnp.concatenate([a_high, a_low], 1), jnp.concatenate([b_high, b_high], 0))
        return r + dot(a_high, b_low)
    return (dot(a_high, b_high) + dot(a_low, b_high)) + dot(a_high, b_low)


def places(size):
    r = lax.broadcasted_iota(jnp.int32, (size, size), 0)
    c = lax.broadcasted_iota(jnp.int32, (size, size), 1)
    return r, c


def alternate(a, size):
    return jnp.concatenate([a[i : i + size] for i in range(size, 128, 2 * size)], 0)


def between(upper, lower, size):
    parts = []
    for i in range(0, 64, size):
        parts += [upper[i : i + size], lower[i : i + size]]
    return jnp.concatenate(parts, 0)


def unit_lower_inverses(inners):
    r, c = places(128)
    lane = lax.broadcasted_iota(jnp.int32, (16, 128), 1)
    row = lax.broadcasted_iota(jnp.int32, (16, 128), 0)
    folded = []
    for a in inners:
        f = jnp.zeros((16, 128), F32)
        for b in range(8):
            f = jnp.where(lane // 16 == b, a[16 * b : 16 * b + 16], f)
        folded.append(f)
    inv = [jnp.where(row == lane % 16, 1.0, 0.0)] * len(inners)
    for j in range(15):
        spread = (lane // 16) * 16 + j
        inv = [
            x
            - jnp.where(
                row > j, jnp.take_along_axis(f, spread, axis=1, mode="promise_in_bounds"), 0.0
            )
            * x[j : j + 1]
            for f, x in zip(folded, inv)
        ]
    inv = [jnp.where(r // 16 == c // 16, jnp.concatenate([x] * 8, 0), 0.0) for x in inv]
    zero = jnp.zeros((64, 128), F32)
    for size in (16, 32, 64):
        below = ((r // (2 * size)) == (c // (2 * size))) & ((r // size) != (c // size))
        part = [mm(alternate(jnp.where(below, a, 0.0), size), d) for a, d in zip(inners, inv)]
        low = [
            alternate(d, size) - mm(alternate(d, size), between(zero, m, size))
            for d, m in zip(inv, part)
        ]
        inv = [
            between(
                jnp.concatenate([d[i : i + size] for i in range(0, 128, 2 * size)], 0), x, size
            )
            for d, x in zip(inv, low)
        ]
    return inv


def unit(values):
    return values * lax.rsqrt(jnp.sum(values * values, -1, keepdims=True) + 1e-06)


def silu(a):
    return a / (1.0 + jnp.exp(-a))


def taps(w, rows, scratch, count):
    acc = w[0:1, :] * scratch[5 : 5 + count, :]
    for j in range(1, KCONV):
        acc = acc + w[j : j + 1, :] * scratch[5 + j : 5 + j + count, :]
    return silu(acc)


def columns(h):
    return slice(h * DK, (h + 1) * DK)


def half_of(at, other):
    return 1 - at[3] if other else at[3]


def head_columns(part, half, h):
    return pl.ds(pl.multiple_of((part * H + half * HALF + h) * DK, DK), DK)


HEADS = range(HALF)
FIRST, SECOND = (2, 0), (1, 3)
OWN = FIRST + SECOND


def fetch_kernel(at, x_all, x_far, x_own, sems):
    copies = []
    for g, to in enumerate((x_far, x_own)):
        for p in range(2):
            begin = ((p + 1) * H + half_of(at, g == 0) * HALF) * DK
            cols = pl.ds(pl.multiple_of(begin, HALF * DK), HALF * DK)
            copies.append(
                pltpu.make_async_copy(x_all.at[:, cols], to.at[p], sems.at[2 * g + p])
            )
    for copy in copies:
        copy.start()
    for copy in copies:
        copy.wait()


def mix_kernel(at, x, w, keys_out, values_out, x_out, scratch, *, other):
    half = half_of(at, other)
    for p in range(2):
        for h in HEADS:
            held = scratch.at[p, h]
            held[0:8, :] = jnp.zeros((8, DK), F32)
            held[8 : 8 + ROWS, :] = x[p, :, columns(h)].astype(F32)
            x_out[p, :, columns(h)] = held[8:16, :]
            m = taps(w[:, head_columns(p + 1, half, h)], ROWS, held, ROWS)
            if p == 0:
                keys_out[h] = unit(m)
            else:
                values_out[h] = m


def at_head(h):
    return pl.ds(pl.multiple_of(h * DK, DK), DK)


def picked(at, which):
    if which is None:
        return list(HEADS)
    return [lax.rem(at[2] + d, 4) for d in which]


def rim_of(at, rim, cols):
    first = at[0] + at[1] + at[2] + at[3] == 0
    return jnp.where(first, 0.0, rim[:, cols].astype(F32))


def first_rows(rim, x, w, scratch):
    scratch[5:8, :] = rim
    scratch[8:16, :] = x
    return taps(w, 8, scratch, 8)


def local_kernel(
    at, keys_in, values_in, x, w, rim, beta, trans_out, keys_out, solved_out, scratch, *, other, which
):
    half = half_of(at, other)
    heads = picked(at, which)
    n = len(heads)

    def with_rim(p, i, h, rest):
        first = first_rows(
            rim_of(at, rim, head_columns(p + 1, half, h)),
            x[p, :, at_head(h)],
            w[:, head_columns(p + 1, half, h)],
            scratch.at[p, i],
        )
        return jnp.concatenate([unit(first) if p == 0 else first, rest[h, 8:, :]], 0)

    keys = [with_rim(0, i, h, keys_in) for i, h in enumerate(heads)]
    values = [with_rim(1, i, h, values_in) for i, h in enumerate(heads)]
    keys_t = [k.T * beta[pl.ds(half * HALF + h, 1), :] for h, k in zip(heads, keys)]
    r, c = places(128)
    strict = r > c
    top = [jnp.where(strict, mm(k[:128], kt[:, :128]), 0.0) for k, kt in zip(keys, keys_t)]
    below = [mmw(k[128:], kt) for k, kt in zip(keys, keys_t)]
    inner = top + [jnp.where(strict, a[:, 128:], 0.0) for a in below]
    right = [jnp.concatenate([k, v], 1) for k, v in zip(keys, values)]
    inv = unit_lower_inverses(inner)
    first = [mmw(d, x[:128]) for d, x in zip(inv[:n], right)]
    rest = [x[128:] - mmw(a[:, :128], y) for x, a, y in zip(right, below, first)]
    second = [mmw(d, z) for d, z in zip(inv[n:], rest)]
    solved = [jnp.concatenate([a, b], 0) for a, b in zip(first, second)]
    trans = [mmw(kt, y) for kt, y in zip(keys_t, solved)]
    for h in range(n):
        trans_out[h, :, :DK] = jnp.where(r == c, 1.0, 0.0) - trans[h][:, :DK]
        trans_out[h, :, DK:] = trans[h][:, DK:]
        keys_out[h] = keys_t[h]
        solved_out[h] = solved[h]


def output_kernel(at, x, rim, w, *refs, other, which):
    blocks, (q_out, o_out, token, scratch) = refs[:-4], refs[-4:]
    token[...] = jnp.zeros_like(token)
    half = half_of(at, other)
    size = HALF * 2 // len(blocks)
    keys_t = [blocks[2 * (i // size)].at[i % size] for i in HEADS]
    solved = [blocks[2 * (i // size) + 1].at[i % size] for i in HEADS]
    queries = []
    for i, h in enumerate(picked(at, which)):
        held, cols = scratch.at[i], head_columns(0, half, h)
        held[5:8, :] = rim_of(at, rim, cols)
        held[8 : 8 + ROWS, :] = x[:, cols].astype(F32)
        queries.append(unit(taps(w[:, cols], ROWS, held, ROWS)))
    r, c = places(ROWS)
    scores = [jnp.where(r >= c, mmw(q, keys_t[h][...]), 0.0) for h, q in zip(HEADS, queries)]
    out = [mmw(s, solved[h][...]) for h, s in zip(HEADS, scores)]
    for h in HEADS:
        q_out[h] = queries[h] - out[h][:, :DK]
        o_out[h] = out[h][:, DK:]


def compose(later, earlier):
    m = mmw(later[:, :DK], earlier)
    return jnp.concatenate([m[:, :DK], m[:, DK:] + later[:, DK:]], 1)


def enter(trans, state):
    return mm(trans[:, :DK], state) + trans[:, DK:]


def ordered(own_first, own, other):
    return jnp.where(own_first, other, own), jnp.where(own_first, own, other)


def chip_kernel(at, kept, came, *outs, which):
    for i, (out, j) in enumerate(zip(outs, picked(at, which))):
        out[...] = compose(*ordered(at[3] == 0, kept[i], came[j]))


def y_kernel(at, b0, b2, b1, b3, total, prefixes, held):
    y = at[2]
    for d, block in enumerate((b0, b1, b2, b3)):
        held[lax.rem(y + 4 - d, 4)] = block[...]
    one = held[0]
    two = compose(held[1], one)
    upper = compose(held[3], held[2])
    prefixes[0] = one
    prefixes[1] = two
    prefixes[2] = compose(held[2], two)
    total[...] = compose(upper, two)


def x_kernel(at, b0, b1, b3, b2, total, prefix, held):
    x = at[1]
    for d, block in enumerate((b0, b1, b2, b3)):
        held[lax.rem(x + 4 - d, 4)] = block[...]
    one = held[0]
    two = compose(held[1], one)
    upper = compose(held[3], held[2])
    three = compose(held[2], two)
    r, c = places(DK)
    none = jnp.concatenate([jnp.where(r == c, 1.0, 0.0), jnp.zeros((DK, DK), F32)], 1)
    prefix[...] = jnp.where(
        x < 2, jnp.where(x == 0, none, one), jnp.where(x == 2, two, three)
    )
    total[...] = compose(upper, two)


def prefix_kernel(at, x_prefix, y_prefixes, out):
    out[0] = x_prefix[...]
    for i in range(3):
        out[i + 1] = compose(y_prefixes[i], x_prefix[...])


def z_kernel(at, b1, b3, b2, prefixes, s0, s1, s2, s3, states):
    y, z = at[2], at[0]
    state = jnp.where(z >= 3, b3[:, DK:], 0.0)
    state = jnp.where(z >= 2, enter(b2[...], state), 0.0)
    state = jnp.where(z >= 1, enter(b1[...], state), 0.0)
    for i in range(4):
        states[i] = enter(prefixes[i], state)
    for d, out in enumerate((s0, s1, s2, s3)):
        out[...] = states[lax.rem(y + d, 4)]


def core_kernel(at, kept_a, kept_b, came, s0, s2, s1, s3, stays, goes):
    y, low = at[2], at[3] == 0
    own = kept_a[1], kept_b[1], kept_a[0], kept_b[0]
    for d, state in enumerate((s0, s1, s2, s3)):
        j = lax.rem(y + 4 - d, 4)
        first = state[...]
        second = enter(jnp.where(low, own[d], came[j]), first)
        stays[j] = jnp.where(low, first, second)
        goes[j] = jnp.where(low, second, first)


def finished(q, o, s, gain, i, h):
    r = mm(q[i], s[h]) + o[i]
    return (r * lax.rsqrt(jnp.mean(r * r, -1, keepdims=True) + 1e-06) * gain[...]).astype(BF16)


def final_own_kernel(at, q, o, s, gain, out):
    for i, h in enumerate(picked(at, OWN)):
        out[:, at_head(h)] = finished(q, o, s, gain, i, h)


def final_kernel(at, q, o, s, gain, own, out):
    for h in HEADS:
        out[:, head_columns(0, at[3], h)] = own[:, columns(h)]
        out[:, head_columns(0, 1 - at[3], h)] = finished(q, o, s, gain, h, h)


class Place:
    def __getitem__(self, i):
        return lax.axis_index(ALL[i])


def step(kernel, args, outs, scratch=(), after=(), vmem=VMEM_BYTES, hbm=(), flops=10**6):
    args, after, hbm = list(args), list(after), list(hbm)

    def body(*refs):
        kernel(Place(), *refs[: len(args) + len(hbm)], *refs[len(args) + len(hbm) + len(after) :])

    anywhere = pl.BlockSpec(memory_space=pl.ANY)
    return pl.pallas_call(
        body,
        in_specs=[pl.BlockSpec()] * len(args) + [anywhere] * (len(hbm) + len(after)),
        out_shape=list(outs),
        scratch_shapes=list(scratch),
        cost_estimate=pl.CostEstimate(flops=flops, bytes_accessed=2**10, transcendentals=0),
        compiler_params=pltpu.CompilerParams(vmem_limit_bytes=vmem),
    )(*args, *hbm, *after)


def shaped(*shape):
    return jax.ShapeDtypeStruct(shape, F32)


def fetch_call(projected):
    x = jax.ShapeDtypeStruct((2, ROWS, HALF * DK), BF16)
    return step(
        fetch_kernel,
        (),
        [x, x],
        [pltpu.SemaphoreType.DMA((4,))],
        vmem=FETCH_BYTES,
        hbm=(projected,),
        flops=FETCH_FLOPS,
    )


def mix_call(x, weight, other):
    return step(
        functools.partial(mix_kernel, other=other),
        (x, weight),
        [shaped(HALF, ROWS, DK)] * 2 + [shaped(2, 8, HALF * DK)],
        [pltpu.VMEM((2, HALF, ROWS + 8, DK), F32)],
    )


def local_call(mixes, weight, rim, beta, other, which=None, after=()):
    n = HALF if which is None else len(which)
    outs = [shaped(n, DK, 2 * DK), shaped(n, DK, ROWS), shaped(n, ROWS, 2 * DK)]
    return step(
        functools.partial(local_kernel, other=other, which=which),
        (*mixes, weight, rim, beta),
        outs,
        [pltpu.VMEM((2, n, 16, DK), F32)],
        after,
    )


def output_call(projected, rim, weight, blocks, other, which=None):
    outs = [shaped(HALF, ROWS, DK), shaped(HALF, ROWS, DK), shaped(8, DK)]
    return step(
        functools.partial(output_kernel, other=other, which=which),
        (projected, rim, weight, *blocks),
        outs,
        [pltpu.VMEM((HALF, ROWS + 8, DK), F32)],
    )


def swap(block):
    return lax.ppermute(block, "core", [(0, 1), (1, 0)])


def shift(block, axis, distance):
    n = lax.axis_size(axis)
    return lax.ppermute(block, axis, [(i, (i + distance) % n) for i in range(n)])


def ring_of(blocks, axis):
    return [shift(block, axis, d + 1) for d, block in enumerate(blocks)]


def shards(projected, weight, beta, gain):
    gain = gain.reshape(1, DK)
    one, state = shaped(DK, 2 * DK), shaped(DK, DK)

    x_far, x_own = fetch_call(projected)
    last = projected[ROWS - (KCONV - 1) :]
    count = lax.axis_size(ALL)
    rim = lax.ppermute(last, ALL, [(i, (i + 1) % count) for i in range(count)])
    mixes_far = mix_call(x_far, weight, True)
    mixes_own = mix_call(x_own, weight, False)
    sent, *far = local_call(mixes_far, weight, rim, beta, True, after=mixes_own[2:])
    came = swap(sent)
    kept_a, *own_a = local_call(mixes_own, weight, rim, beta, False, FIRST)
    chip_a = functools.partial(chip_kernel, which=FIRST)
    across, own = step(chip_a, (kept_a, came), [one, one])
    first, across = across, shift(across, "y", 2)
    kept_b, *own_b = local_call(mixes_own, weight, rim, beta, False, SECOND, (first,))
    chip_b = functools.partial(chip_kernel, which=SECOND)
    after, before = step(chip_b, (kept_b, came), [one, one])

    held = pltpu.VMEM((4, DK, 2 * DK), F32)
    b1, b2, b3 = shift(after, "y", 1), across, shift(before, "y", 3)
    q_far, o_far, far_done = output_call(projected, rim, weight, far, True)
    q_own, o_own, own_done = output_call(projected, rim, weight, own_a + own_b, False, OWN)
    trans, y_prefixes = step(
        y_kernel,
        (own, b2, b1, b3),
        [one, shaped(3, DK, 2 * DK)],
        [held],
        (far_done, own_done),
    )
    b1, b2, b3 = ring_of([trans] * 3, "x")
    trans, x_prefix = step(x_kernel, (trans, b1, b3, b2), [one, one], [held])
    b1, b2, b3 = ring_of([trans] * 3, "z")
    (prefixes,) = step(prefix_kernel, (x_prefix, y_prefixes), [shaped(4, DK, 2 * DK)])

    states = step(
        z_kernel,
        (b1, b3, b2, prefixes),
        [state] * 4,
        [pltpu.VMEM((4, DK, DK), F32)],
    )
    s1, s2, s3 = ring_of(states[1:], "y")
    s_own, goes = step(core_kernel, (kept_a, kept_b, came, states[0], s2, s1, s3), [shaped(HALF, DK, DK)] * 2)
    s_far = swap(goes)
    half = jax.ShapeDtypeStruct((ROWS, HALF * DK), BF16)
    (own,) = step(final_own_kernel, (q_own, o_own, s_own, gain), [half])
    out = jax.ShapeDtypeStruct((ROWS, H * DK), BF16)
    return step(final_kernel, (q_far, o_far, s_far, gain, own), [out])[0]


def solution(mesh):
    grid = Mesh(mesh.devices.reshape(4, 4, 4, 2), ALL)
    placed = (P(ALL, None), P(), P(None, ALL), P())
    return jax.shard_map(
        shards, mesh=grid, in_specs=placed, out_specs=P(ALL, None), check_vma=False
    )
```

```python
import functools

import jax
import jax.numpy as jnp
from jax import lax
from jax.experimental import pallas as pl
from jax.experimental.pallas import tpu as pltpu
from jax.sharding import Mesh
from jax.sharding import PartitionSpec as P

H = 8
DK = 128
KCONV = 4
HALF = H // 2
ROWS = 256
F32, BF16 = jnp.float32, jnp.bfloat16
ALL = ("z", "x", "y", "core")
VMEM_BYTES = 48 * 1024 * 1024
FETCH_BYTES = 52 * 1024 * 1024
FETCH_FLOPS = 10**9


def split(a):
    high = a.astype(BF16)
    return high, (a - high.astype(F32)).astype(BF16)


def dot(a, b):
    return jnp.dot(a, b, preferred_element_type=F32)


def mm(a, b):
    a_high, a_low = split(a)
    b_high, b_low = split(b)
    wide = jnp.concatenate([b_high, b_low], 1)
    r = dot(jnp.concatenate([a_high, a_low], 1), jnp.concatenate([wide, wide], 0))
    n = b.shape[1]
    return r[:, :n] + r[:, n:]


def mmw(a, b):
    a_high, a_low = split(a)
    b_high, b_low = split(b)
    if a.shape[1] == 128:
        r = dot(jnp.concatenate([a_high, a_low], 1), jnp.concatenate([b_high, b_high], 0))
        return r + dot(a_high, b_low)
    return (dot(a_high, b_high) + dot(a_low, b_high)) + dot(a_high, b_low)


def places(size):
    r = lax.broadcasted_iota(jnp.int32, (size, size), 0)
    c = lax.broadcasted_iota(jnp.int32, (size, size), 1)
    return r, c


def alternate(a, size):
    return jnp.concatenate([a[i : i + size] for i in range(size, 128, 2 * size)], 0)


def between(upper, lower, size):
    parts = []
    for i in range(0, 64, size):
        parts += [upper[i : i + size], lower[i : i + size]]
    return jnp.concatenate(parts, 0)


def unit_lower_inverses(inners):
    r, c = places(128)
    lane = lax.broadcasted_iota(jnp.int32, (16, 128), 1)
    row = lax.broadcasted_iota(jnp.int32, (16, 128), 0)
    folded = []
    for a in inners:
        f = jnp.zeros((16, 128), F32)
        for b in range(8):
            f = jnp.where(lane // 16 == b, a[16 * b : 16 * b + 16], f)
        folded.append(f)
    inv = [jnp.where(row == lane % 16, 1.0, 0.0)] * len(inners)
    for j in range(15):
        spread = (lane // 16) * 16 + j
        inv = [
            x
            - jnp.where(
                row > j, jnp.take_along_axis(f, spread, axis=1, mode="promise_in_bounds"), 0.0
            )
            * x[j : j + 1]
            for f, x in zip(folded, inv)
        ]
    inv = [jnp.where(r // 16 == c // 16, jnp.concatenate([x] * 8, 0), 0.0) for x in inv]
    zero = jnp.zeros((64, 128), F32)
    for size in (16, 32, 64):
        below = ((r // (2 * size)) == (c // (2 * size))) & ((r // size) != (c // size))
        part = [mm(alternate(jnp.where(below, a, 0.0), size), d) for a, d in zip(inners, inv)]
        low = [
            alternate(d, size) - mm(alternate(d, size), between(zero, m, size))
            for d, m in zip(inv, part)
        ]
        inv = [
            between(
                jnp.concatenate([d[i : i + size] for i in range(0, 128, 2 * size)], 0), x, size
            )
            for d, x in zip(inv, low)
        ]
    return inv


def unit(values):
    return values * lax.rsqrt(jnp.sum(values * values, -1, keepdims=True) + 1e-06)


def silu(a):
    return a / (1.0 + jnp.exp(-a))


def taps(w, rows, scratch, count):
    acc = w[0:1, :] * scratch[5 : 5 + count, :]
    for j in range(1, KCONV):
        acc = acc + w[j : j + 1, :] * scratch[5 + j : 5 + j + count, :]
    return silu(acc)


def columns(h):
    return slice(h * DK, (h + 1) * DK)


def half_of(at, other):
    return 1 - at[3] if other else at[3]


def head_columns(part, half, h):
    return pl.ds(pl.multiple_of((part * H + half * HALF + h) * DK, DK), DK)


HEADS = range(HALF)
FIRST, SECOND = (2, 0), (1, 3)
OWN = FIRST + SECOND


def fetch_kernel(at, x_all, x_far, x_own, sems):
    copies = []
    for g, to in enumerate((x_far, x_own)):
        for p in range(2):
            begin = ((p + 1) * H + half_of(at, g == 0) * HALF) * DK
            cols = pl.ds(pl.multiple_of(begin, HALF * DK), HALF * DK)
            copies.append(
                pltpu.make_async_copy(x_all.at[:, cols], to.at[p], sems.at[2 * g + p])
            )
    for copy in copies:
        copy.start()
    for copy in copies:
        copy.wait()


def mix_kernel(at, x, w, keys_out, values_out, x_out, scratch, *, other):
    half = half_of(at, other)
    for p in range(2):
        for h in HEADS:
            held = scratch.at[p, h]
            held[0:8, :] = jnp.zeros((8, DK), F32)
            held[8 : 8 + ROWS, :] = x[p, :, columns(h)].astype(F32)
            x_out[p, :, columns(h)] = held[8:16, :]
            m = taps(w[:, head_columns(p + 1, half, h)], ROWS, held, ROWS)
            if p == 0:
                keys_out[h] = unit(m)
            else:
                values_out[h] = m


def at_head(h):
    return pl.ds(pl.multiple_of(h * DK, DK), DK)


def picked(at, which):
    if which is None:
        return list(HEADS)
    return [lax.rem(at[2] + d, 4) for d in which]


def rim_of(at, rim, cols):
    first = at[0] + at[1] + at[2] + at[3] == 0
    return jnp.where(first, 0.0, rim[:, cols].astype(F32))


def first_rows(rim, x, w, scratch):
    scratch[5:8, :] = rim
    scratch[8:16, :] = x
    return taps(w, 8, scratch, 8)


def local_kernel(
    at, keys_in, values_in, x, w, rim, beta, trans_out, keys_out, solved_out, scratch, *, other, which
):
    half = half_of(at, other)
    heads = picked(at, which)
    n = len(heads)

    def with_rim(p, i, h, rest):
        first = first_rows(
            rim_of(at, rim, head_columns(p + 1, half, h)),
            x[p, :, at_head(h)],
            w[:, head_columns(p + 1, half, h)],
            scratch.at[p, i],
        )
        return jnp.concatenate([unit(first) if p == 0 else first, rest[h, 8:, :]], 0)

    keys = [with_rim(0, i, h, keys_in) for i, h in enumerate(heads)]
    values = [with_rim(1, i, h, values_in) for i, h in enumerate(heads)]
    keys_t = [k.T * beta[pl.ds(half * HALF + h, 1), :] for h, k in zip(heads, keys)]
    r, c = places(128)
    strict = r > c
    top = [jnp.where(strict, mm(k[:128], kt[:, :128]), 0.0) for k, kt in zip(keys, keys_t)]
    below = [mmw(k[128:], kt) for k, kt in zip(keys, keys_t)]
    inner = top + [jnp.where(strict, a[:, 128:], 0.0) for a in below]
    right = [jnp.concatenate([k, v], 1) for k, v in zip(keys, values)]
    inv = unit_lower_inverses(inner)
    first = [mmw(d, x[:128]) for d, x in zip(inv[:n], right)]
    rest = [x[128:] - mmw(a[:, :128], y) for x, a, y in zip(right, below, first)]
    second = [mmw(d, z) for d, z in zip(inv[n:], rest)]
    solved = [jnp.concatenate([a, b], 0) for a, b in zip(first, second)]
    trans = [mmw(kt, y) for kt, y in zip(keys_t, solved)]
    for h in range(n):
        trans_out[h, :, :DK] = jnp.where(r == c, 1.0, 0.0) - trans[h][:, :DK]
        trans_out[h, :, DK:] = trans[h][:, DK:]
        keys_out[h] = keys_t[h]
        solved_out[h] = solved[h]


def output_kernel(at, x, rim, w, *refs, other, which):
    blocks, (q_out, o_out, token, scratch) = refs[:-4], refs[-4:]
    token[...] = jnp.zeros_like(token)
    half = half_of(at, other)
    size = HALF * 2 // len(blocks)
    keys_t = [blocks[2 * (i // size)].at[i % size] for i in HEADS]
    solved = [blocks[2 * (i // size) + 1].at[i % size] for i in HEADS]
    queries = []
    for i, h in enumerate(picked(at, which)):
        held, cols = scratch.at[i], head_columns(0, half, h)
        held[5:8, :] = rim_of(at, rim, cols)
        held[8 : 8 + ROWS, :] = x[:, cols].astype(F32)
        queries.append(unit(taps(w[:, cols], ROWS, held, ROWS)))
    r, c = places(ROWS)
    scores = [jnp.where(r >= c, mmw(q, keys_t[h][...]), 0.0) for h, q in zip(HEADS, queries)]
    out = [mmw(s, solved[h][...]) for h, s in zip(HEADS, scores)]
    for h in HEADS:
        q_out[h] = queries[h] - out[h][:, :DK]
        o_out[h] = out[h][:, DK:]


def compose(later, earlier):
    m = mmw(later[:, :DK], earlier)
    return jnp.concatenate([m[:, :DK], m[:, DK:] + later[:, DK:]], 1)


def enter(trans, state):
    return mm(trans[:, :DK], state) + trans[:, DK:]


def ordered(own_first, own, other):
    return jnp.where(own_first, other, own), jnp.where(own_first, own, other)


def chip_kernel(at, kept, came, *outs, which):
    for i, (out, j) in enumerate(zip(outs, picked(at, which))):
        out[...] = compose(*ordered(at[3] == 0, kept[i], came[j]))


def y_kernel(at, b0, b2, b1, b3, total, prefixes, held):
    y = at[2]
    for d, block in enumerate((b0, b1, b2, b3)):
        held[lax.rem(y + 4 - d, 4)] = block[...]
    one = held[0]
    two = compose(held[1], one)
    upper = compose(held[3], held[2])
    prefixes[0] = one
    prefixes[1] = two
    prefixes[2] = compose(held[2], two)
    total[...] = compose(upper, two)


def x_kernel(at, b0, b1, b3, b2, total, prefix, held):
    x = at[1]
    for d, block in enumerate((b0, b1, b2, b3)):
        held[lax.rem(x + 4 - d, 4)] = block[...]
    one = held[0]
    two = compose(held[1], one)
    upper = compose(held[3], held[2])
    three = compose(held[2], two)
    r, c = places(DK)
    none = jnp.concatenate([jnp.where(r == c, 1.0, 0.0), jnp.zeros((DK, DK), F32)], 1)
    prefix[...] = jnp.where(
        x < 2, jnp.where(x == 0, none, one), jnp.where(x == 2, two, three)
    )
    total[...] = compose(upper, two)


def prefix_kernel(at, x_prefix, y_prefixes, out):
    out[0] = x_prefix[...]
    for i in range(3):
        out[i + 1] = compose(y_prefixes[i], x_prefix[...])


def z_kernel(at, b1, b3, b2, prefixes, s0, s1, s2, s3, states):
    y, z = at[2], at[0]
    state = jnp.where(z >= 3, b3[:, DK:], 0.0)
    state = jnp.where(z >= 2, enter(b2[...], state), 0.0)
    state = jnp.where(z >= 1, enter(b1[...], state), 0.0)
    for i in range(4):
        states[i] = enter(prefixes[i], state)
    for d, out in enumerate((s0, s1, s2, s3)):
        out[...] = states[lax.rem(y + d, 4)]


def core_kernel(at, kept_a, kept_b, came, s0, s2, s1, s3, stays, goes):
    y, low = at[2], at[3] == 0
    own = kept_a[1], kept_b[1], kept_a[0], kept_b[0]
    for d, state in enumerate((s0, s1, s2, s3)):
        j = lax.rem(y + 4 - d, 4)
        first = state[...]
        second = enter(jnp.where(low, own[d], came[j]), first)
        stays[j] = jnp.where(low, first, second)
        goes[j] = jnp.where(low, second, first)


def finished(q, o, s, gain, i, h):
    r = mm(q[i], s[h]) + o[i]
    return (r * lax.rsqrt(jnp.mean(r * r, -1, keepdims=True) + 1e-06) * gain[...]).astype(BF16)


def final_own_kernel(at, q, o, s, gain, out):
    for i, h in enumerate(picked(at, OWN)):
        out[:, at_head(h)] = finished(q, o, s, gain, i, h)


def final_kernel(at, q, o, s, gain, own, out, far, sems):
    def copy(part, half, h, count, i):
        cols = pl.ds(pl.multiple_of((half * HALF + h) * DK, count * DK), count * DK)
        return pltpu.make_async_copy(part, out.at[:, cols], sems.at[i])

    copies = [copy(own, at[3], 0, HALF, 0)]
    copies[0].start()
    for i in range(2):
        for h in (2 * i, 2 * i + 1):
            far[i, :, columns(h - 2 * i)] = finished(q, o, s, gain, h, h)
        copies.append(copy(far.at[i], 1 - at[3], 2 * i, 2, 1 + i))
        copies[-1].start()
    for c in copies:
        c.wait()


class Place:
    def __getitem__(self, i):
        return lax.axis_index(ALL[i])


def step(kernel, args, outs, scratch=(), after=(), vmem=VMEM_BYTES, hbm=(), flops=10**6, out=None):
    args, after, hbm = list(args), list(after), list(hbm)

    def body(*refs):
        kernel(Place(), *refs[: len(args) + len(hbm)], *refs[len(args) + len(hbm) + len(after) :])

    anywhere = pl.BlockSpec(memory_space=pl.ANY)
    return pl.pallas_call(
        body,
        in_specs=[pl.BlockSpec()] * len(args) + [anywhere] * (len(hbm) + len(after)),
        out_specs=[pl.BlockSpec() if out is None else out] * len(outs),
        out_shape=list(outs),
        scratch_shapes=list(scratch),
        cost_estimate=pl.CostEstimate(flops=flops, bytes_accessed=2**10, transcendentals=0),
        compiler_params=pltpu.CompilerParams(vmem_limit_bytes=vmem),
    )(*args, *hbm, *after)


def shaped(*shape):
    return jax.ShapeDtypeStruct(shape, F32)


def fetch_call(projected):
    x = jax.ShapeDtypeStruct((2, ROWS, HALF * DK), BF16)
    return step(
        fetch_kernel,
        (),
        [x, x],
        [pltpu.SemaphoreType.DMA((4,))],
        vmem=FETCH_BYTES,
        hbm=(projected,),
        flops=FETCH_FLOPS,
    )


def mix_call(x, weight, other):
    return step(
        functools.partial(mix_kernel, other=other),
        (x, weight),
        [shaped(HALF, ROWS, DK)] * 2 + [shaped(2, 8, HALF * DK)],
        [pltpu.VMEM((2, HALF, ROWS + 8, DK), F32)],
    )


def local_call(mixes, weight, rim, beta, other, which=None, after=()):
    n = HALF if which is None else len(which)
    outs = [shaped(n, DK, 2 * DK), shaped(n, DK, ROWS), shaped(n, ROWS, 2 * DK)]
    return step(
        functools.partial(local_kernel, other=other, which=which),
        (*mixes, weight, rim, beta),
        outs,
        [pltpu.VMEM((2, n, 16, DK), F32)],
        after,
    )


def output_call(projected, rim, weight, blocks, other, which=None):
    outs = [shaped(HALF, ROWS, DK), shaped(HALF, ROWS, DK), shaped(8, DK)]
    return step(
        functools.partial(output_kernel, other=other, which=which),
        (projected, rim, weight, *blocks),
        outs,
        [pltpu.VMEM((HALF, ROWS + 8, DK), F32)],
    )


def swap(block):
    return lax.ppermute(block, "core", [(0, 1), (1, 0)])


def shift(block, axis, distance):
    n = lax.axis_size(axis)
    return lax.ppermute(block, axis, [(i, (i + distance) % n) for i in range(n)])


def ring_of(blocks, axis):
    return [shift(block, axis, d + 1) for d, block in enumerate(blocks)]


def shards(projected, weight, beta, gain):
    gain = gain.reshape(1, DK)
    one, state = shaped(DK, 2 * DK), shaped(DK, DK)

    x_far, x_own = fetch_call(projected)
    last = projected[ROWS - (KCONV - 1) :]
    count = lax.axis_size(ALL)
    rim = lax.ppermute(last, ALL, [(i, (i + 1) % count) for i in range(count)])
    mixes_far = mix_call(x_far, weight, True)
    mixes_own = mix_call(x_own, weight, False)
    sent, *far = local_call(mixes_far, weight, rim, beta, True, after=mixes_own[2:])
    came = swap(sent)
    kept_a, *own_a = local_call(mixes_own, weight, rim, beta, False, FIRST)
    chip_a = functools.partial(chip_kernel, which=FIRST)
    across, own = step(chip_a, (kept_a, came), [one, one])
    first, across = across, shift(across, "y", 2)
    kept_b, *own_b = local_call(mixes_own, weight, rim, beta, False, SECOND, (first,))
    chip_b = functools.partial(chip_kernel, which=SECOND)
    after, before = step(chip_b, (kept_b, came), [one, one])

    held = pltpu.VMEM((4, DK, 2 * DK), F32)
    b1, b2, b3 = shift(after, "y", 1), across, shift(before, "y", 3)
    q_far, o_far, far_done = output_call(projected, rim, weight, far, True)
    q_own, o_own, own_done = output_call(projected, rim, weight, own_a + own_b, False, OWN)
    trans, y_prefixes = step(
        y_kernel,
        (own, b2, b1, b3),
        [one, shaped(3, DK, 2 * DK)],
        [held],
        (far_done,),
    )
    b1, b2, b3 = ring_of([trans] * 3, "x")
    trans, x_prefix = step(x_kernel, (trans, b1, b3, b2), [one, one], [held], (own_done,))
    b1, b2, b3 = ring_of([trans] * 3, "z")
    (prefixes,) = step(prefix_kernel, (x_prefix, y_prefixes), [shaped(4, DK, 2 * DK)])

    states = step(
        z_kernel,
        (b1, b3, b2, prefixes),
        [state] * 4,
        [pltpu.VMEM((4, DK, DK), F32)],
    )
    s1, s2, s3 = ring_of(states[1:], "y")
    s_own, goes = step(core_kernel, (kept_a, kept_b, came, states[0], s2, s1, s3), [shaped(HALF, DK, DK)] * 2)
    s_far = swap(goes)
    half = jax.ShapeDtypeStruct((ROWS, HALF * DK), BF16)
    (own,) = step(final_own_kernel, (q_own, o_own, s_own, gain), [half])
    out = jax.ShapeDtypeStruct((ROWS, H * DK), BF16)
    (out,) = step(
        final_kernel,
        (q_far, o_far, s_far, gain, own),
        [out],
        [pltpu.VMEM((2, ROWS, 2 * DK), BF16), pltpu.SemaphoreType.DMA((3,))],
        out=pl.BlockSpec(memory_space=pl.ANY),
    )
    return out


def solution(mesh):
    grid = Mesh(mesh.devices.reshape(4, 4, 4, 2), ALL)
    placed = (P(ALL, None), P(), P(None, ALL), P())
    return jax.shard_map(
        shards, mesh=grid, in_specs=placed, out_specs=P(ALL, None), check_vma=False
    )
```

```python
import functools

import jax
import jax.numpy as jnp
from jax import lax
from jax.experimental import pallas as pl
from jax.experimental.pallas import tpu as pltpu
from jax.sharding import Mesh
from jax.sharding import PartitionSpec as P

H = 8
DK = 128
KCONV = 4
HALF = H // 2
ROWS = 256
F32, BF16 = jnp.float32, jnp.bfloat16
ALL = ("z", "x", "y", "core")
VMEM_BYTES = 48 * 1024 * 1024
FETCH_BYTES = 52 * 1024 * 1024
FETCH_FLOPS = 10**9


def split(a):
    high = a.astype(BF16)
    return high, (a - high.astype(F32)).astype(BF16)


def dot(a, b):
    return jnp.dot(a, b, preferred_element_type=F32)


def mm(a, b):
    a_high, a_low = split(a)
    b_high, b_low = split(b)
    wide = jnp.concatenate([b_high, b_low], 1)
    r = dot(jnp.concatenate([a_high, a_low], 1), jnp.concatenate([wide, wide], 0))
    n = b.shape[1]
    return r[:, :n] + r[:, n:]


def mmw(a, b):
    a_high, a_low = split(a)
    b_high, b_low = split(b)
    if a.shape[1] == 128:
        r = dot(jnp.concatenate([a_high, a_low], 1), jnp.concatenate([b_high, b_high], 0))
        return r + dot(a_high, b_low)
    return (dot(a_high, b_high) + dot(a_low, b_high)) + dot(a_high, b_low)


def places(size):
    r = lax.broadcasted_iota(jnp.int32, (size, size), 0)
    c = lax.broadcasted_iota(jnp.int32, (size, size), 1)
    return r, c


def alternate(a, size):
    return jnp.concatenate([a[i : i + size] for i in range(size, 128, 2 * size)], 0)


def between(upper, lower, size):
    parts = []
    for i in range(0, 64, size):
        parts += [upper[i : i + size], lower[i : i + size]]
    return jnp.concatenate(parts, 0)


def unit_lower_inverses(inners):
    r, c = places(128)
    lane = lax.broadcasted_iota(jnp.int32, (16, 128), 1)
    row = lax.broadcasted_iota(jnp.int32, (16, 128), 0)
    folded = []
    for a in inners:
        f = jnp.zeros((16, 128), F32)
        for b in range(8):
            f = jnp.where(lane // 16 == b, a[16 * b : 16 * b + 16], f)
        folded.append(f)
    inv = [jnp.where(row == lane % 16, 1.0, 0.0)] * len(inners)
    for j in range(15):
        spread = (lane // 16) * 16 + j
        inv = [
            x - jnp.take_along_axis(f, spread, axis=1, mode="promise_in_bounds") * x[j : j + 1]
            for f, x in zip(folded, inv)
        ]
    inv = [jnp.where(r // 16 == c // 16, jnp.concatenate([x] * 8, 0), 0.0) for x in inv]
    zero = jnp.zeros((64, 128), F32)
    for size in (16, 32, 64):
        below = ((r // (2 * size)) == (c // (2 * size))) & ((r // size) != (c // size))
        part = [mm(alternate(jnp.where(below, a, 0.0), size), d) for a, d in zip(inners, inv)]
        low = [
            alternate(d, size) - mm(alternate(d, size), between(zero, m, size))
            for d, m in zip(inv, part)
        ]
        inv = [
            between(
                jnp.concatenate([d[i : i + size] for i in range(0, 128, 2 * size)], 0), x, size
            )
            for d, x in zip(inv, low)
        ]
    return inv


def unit(values):
    return values * lax.rsqrt(jnp.sum(values * values, -1, keepdims=True) + 1e-06)


def silu(a):
    return a / (1.0 + jnp.exp(-a))


def taps(w, rows, scratch, count):
    acc = w[0:1, :] * scratch[5 : 5 + count, :]
    for j in range(1, KCONV):
        acc = acc + w[j : j + 1, :] * scratch[5 + j : 5 + j + count, :]
    return silu(acc)


def columns(h):
    return slice(h * DK, (h + 1) * DK)


def half_of(at, other):
    return 1 - at[3] if other else at[3]


def head_columns(part, half, h):
    return pl.ds(pl.multiple_of((part * H + half * HALF + h) * DK, DK), DK)


HEADS = range(HALF)
FIRST, SECOND = (2, 0), (1, 3)
OWN = FIRST + SECOND


def fetch_kernel(at, x_all, x_far, x_own, sems):
    copies = []
    for g, to in enumerate((x_far, x_own)):
        for p in range(2):
            begin = ((p + 1) * H + half_of(at, g == 0) * HALF) * DK
            cols = pl.ds(pl.multiple_of(begin, HALF * DK), HALF * DK)
            copies.append(
                pltpu.make_async_copy(x_all.at[:, cols], to.at[p], sems.at[2 * g + p])
            )
    for copy in copies:
        copy.start()
    for copy in copies:
        copy.wait()


def mix_kernel(at, x, w, keys_out, values_out, x_out, scratch, *, other):
    half = half_of(at, other)
    for p in range(2):
        for h in HEADS:
            held = scratch.at[p, h]
            held[0:8, :] = jnp.zeros((8, DK), F32)
            held[8 : 8 + ROWS, :] = x[p, :, columns(h)].astype(F32)
            x_out[p, :, columns(h)] = held[8:16, :]
            m = taps(w[:, head_columns(p + 1, half, h)], ROWS, held, ROWS)
            if p == 0:
                keys_out[h] = unit(m)
            else:
                values_out[h] = m


def at_head(h):
    return pl.ds(pl.multiple_of(h * DK, DK), DK)


def picked(at, which):
    if which is None:
        return list(HEADS)
    return [lax.rem(at[2] + d, 4) for d in which]


def rim_of(at, rim, cols):
    first = at[0] + at[1] + at[2] + at[3] == 0
    return jnp.where(first, 0.0, rim[:, cols].astype(F32))


def first_rows(rim, x, w, scratch):
    scratch[5:8, :] = rim
    scratch[8:16, :] = x
    return taps(w, 8, scratch, 8)


def local_kernel(
    at, keys_in, values_in, x, w, rim, beta, trans_out, keys_out, solved_out, scratch, *, other, which
):
    half = half_of(at, other)
    heads = picked(at, which)
    n = len(heads)

    def with_rim(p, i, h, rest):
        first = first_rows(
            rim_of(at, rim, head_columns(p + 1, half, h)),
            x[p, :, at_head(h)],
            w[:, head_columns(p + 1, half, h)],
            scratch.at[p, i],
        )
        return jnp.concatenate([unit(first) if p == 0 else first, rest[h, 8:, :]], 0)

    keys = [with_rim(0, i, h, keys_in) for i, h in enumerate(heads)]
    values = [with_rim(1, i, h, values_in) for i, h in enumerate(heads)]
    keys_t = [k.T * beta[pl.ds(half * HALF + h, 1), :] for h, k in zip(heads, keys)]
    r, c = places(128)
    strict = r > c
    top = [jnp.where(strict, mm(k[:128], kt[:, :128]), 0.0) for k, kt in zip(keys, keys_t)]
    below = [mmw(k[128:], kt) for k, kt in zip(keys, keys_t)]
    inner = top + [jnp.where(strict, a[:, 128:], 0.0) for a in below]
    right = [jnp.concatenate([k, v], 1) for k, v in zip(keys, values)]
    inv = unit_lower_inverses(inner)
    first = [mmw(d, x[:128]) for d, x in zip(inv[:n], right)]
    rest = [x[128:] - mmw(a[:, :128], y) for x, a, y in zip(right, below, first)]
    second = [mmw(d, z) for d, z in zip(inv[n:], rest)]
    solved = [jnp.concatenate([a, b], 0) for a, b in zip(first, second)]
    trans = [mmw(kt, y) for kt, y in zip(keys_t, solved)]
    for h in range(n):
        trans_out[h, :, :DK] = jnp.where(r == c, 1.0, 0.0) - trans[h][:, :DK]
        trans_out[h, :, DK:] = trans[h][:, DK:]
        keys_out[h] = keys_t[h]
        solved_out[h] = solved[h]


def output_kernel(at, x, rim, w, *refs, other, which):
    blocks, (q_out, o_out, token, scratch) = refs[:-4], refs[-4:]
    token[...] = jnp.zeros_like(token)
    half = half_of(at, other)
    size = HALF * 2 // len(blocks)
    keys_t = [blocks[2 * (i // size)].at[i % size] for i in HEADS]
    solved = [blocks[2 * (i // size) + 1].at[i % size] for i in HEADS]
    queries = []
    for i, h in enumerate(picked(at, which)):
        held, cols = scratch.at[i], head_columns(0, half, h)
        held[5:8, :] = rim_of(at, rim, cols)
        held[8 : 8 + ROWS, :] = x[:, cols].astype(F32)
        queries.append(unit(taps(w[:, cols], ROWS, held, ROWS)))
    r, c = places(ROWS)
    scores = [jnp.where(r >= c, mmw(q, keys_t[h][...]), 0.0) for h, q in zip(HEADS, queries)]
    out = [mmw(s, solved[h][...]) for h, s in zip(HEADS, scores)]
    for h in HEADS:
        q_out[h] = queries[h] - out[h][:, :DK]
        o_out[h] = out[h][:, DK:]


def compose(later, earlier):
    m = mmw(later[:, :DK], earlier)
    return jnp.concatenate([m[:, :DK], m[:, DK:] + later[:, DK:]], 1)


def enter(trans, state):
    return mm(trans[:, :DK], state) + trans[:, DK:]


def ordered(own_first, own, other):
    return jnp.where(own_first, other, own), jnp.where(own_first, own, other)


def chip_kernel(at, kept, came, *outs, which):
    for i, (out, j) in enumerate(zip(outs, picked(at, which))):
        out[...] = compose(*ordered(at[3] == 0, kept[i], came[j]))


def y_kernel(at, b0, b2, b1, b3, total, prefixes, held):
    y = at[2]
    for d, block in enumerate((b0, b1, b2, b3)):
        held[lax.rem(y + 4 - d, 4)] = block[...]
    one = held[0]
    two = compose(held[1], one)
    upper = compose(held[3], held[2])
    prefixes[0] = one
    prefixes[1] = two
    prefixes[2] = compose(held[2], two)
    total[...] = compose(upper, two)


def x_kernel(at, b0, b1, b3, b2, total, prefix, held):
    x = at[1]
    for d, block in enumerate((b0, b1, b2, b3)):
        held[lax.rem(x + 4 - d, 4)] = block[...]
    one = held[0]
    two = compose(held[1], one)
    upper = compose(held[3], held[2])
    three = compose(held[2], two)
    r, c = places(DK)
    none = jnp.concatenate([jnp.where(r == c, 1.0, 0.0), jnp.zeros((DK, DK), F32)], 1)
    prefix[...] = jnp.where(
        x < 2, jnp.where(x == 0, none, one), jnp.where(x == 2, two, three)
    )
    total[...] = compose(upper, two)


def prefix_kernel(at, x_prefix, y_prefixes, out):
    out[0] = x_prefix[...]
    for i in range(3):
        out[i + 1] = compose(y_prefixes[i], x_prefix[...])


def z_kernel(at, b1, b3, b2, prefixes, s0, s1, s2, s3, states):
    y, z = at[2], at[0]
    state = jnp.where(z >= 3, b3[:, DK:], 0.0)
    state = jnp.where(z >= 2, enter(b2[...], state), 0.0)
    state = jnp.where(z >= 1, enter(b1[...], state), 0.0)
    for i in range(4):
        states[i] = enter(prefixes[i], state)
    for d, out in enumerate((s0, s1, s2, s3)):
        out[...] = states[lax.rem(y + d, 4)]


def core_kernel(at, kept_a, kept_b, came, s0, s2, s1, s3, stays, goes):
    y, low = at[2], at[3] == 0
    own = kept_a[1], kept_b[1], kept_a[0], kept_b[0]
    for d, state in enumerate((s0, s1, s2, s3)):
        j = lax.rem(y + 4 - d, 4)
        first = state[...]
        second = enter(jnp.where(low, own[d], came[j]), first)
        stays[j] = jnp.where(low, first, second)
        goes[j] = jnp.where(low, second, first)


def finished(q, o, s, gain, i, h):
    r = mm(q[i], s[h]) + o[i]
    return (r * lax.rsqrt(jnp.mean(r * r, -1, keepdims=True) + 1e-06) * gain[...]).astype(BF16)


def final_own_kernel(at, q, o, s, gain, out):
    for i, h in enumerate(picked(at, OWN)):
        out[:, at_head(h)] = finished(q, o, s, gain, i, h)


def final_kernel(at, q, o, s, gain, own, out):
    for h in HEADS:
        out[:, head_columns(0, at[3], h)] = own[:, columns(h)]
        out[:, head_columns(0, 1 - at[3], h)] = finished(q, o, s, gain, h, h)


class Place:
    def __getitem__(self, i):
        return lax.axis_index(ALL[i])


def step(kernel, args, outs, scratch=(), after=(), vmem=VMEM_BYTES, hbm=(), flops=10**6):
    args, after, hbm = list(args), list(after), list(hbm)

    def body(*refs):
        kernel(Place(), *refs[: len(args) + len(hbm)], *refs[len(args) + len(hbm) + len(after) :])

    anywhere = pl.BlockSpec(memory_space=pl.ANY)
    return pl.pallas_call(
        body,
        in_specs=[pl.BlockSpec()] * len(args) + [anywhere] * (len(hbm) + len(after)),
        out_shape=list(outs),
        scratch_shapes=list(scratch),
        cost_estimate=pl.CostEstimate(flops=flops, bytes_accessed=2**10, transcendentals=0),
        compiler_params=pltpu.CompilerParams(vmem_limit_bytes=vmem),
    )(*args, *hbm, *after)


def shaped(*shape):
    return jax.ShapeDtypeStruct(shape, F32)


def fetch_call(projected):
    x = jax.ShapeDtypeStruct((2, ROWS, HALF * DK), BF16)
    return step(
        fetch_kernel,
        (),
        [x, x],
        [pltpu.SemaphoreType.DMA((4,))],
        vmem=FETCH_BYTES,
        hbm=(projected,),
        flops=FETCH_FLOPS,
    )


def mix_call(x, weight, other):
    return step(
        functools.partial(mix_kernel, other=other),
        (x, weight),
        [shaped(HALF, ROWS, DK)] * 2 + [shaped(2, 8, HALF * DK)],
        [pltpu.VMEM((2, HALF, ROWS + 8, DK), F32)],
    )


def local_call(mixes, weight, rim, beta, other, which=None, after=()):
    n = HALF if which is None else len(which)
    outs = [shaped(n, DK, 2 * DK), shaped(n, DK, ROWS), shaped(n, ROWS, 2 * DK)]
    return step(
        functools.partial(local_kernel, other=other, which=which),
        (*mixes, weight, rim, beta),
        outs,
        [pltpu.VMEM((2, n, 16, DK), F32)],
        after,
    )


def output_call(projected, rim, weight, blocks, other, which=None):
    outs = [shaped(HALF, ROWS, DK), shaped(HALF, ROWS, DK), shaped(8, DK)]
    return step(
        functools.partial(output_kernel, other=other, which=which),
        (projected, rim, weight, *blocks),
        outs,
        [pltpu.VMEM((HALF, ROWS + 8, DK), F32)],
    )


def swap(block):
    return lax.ppermute(block, "core", [(0, 1), (1, 0)])


def shift(block, axis, distance):
    n = lax.axis_size(axis)
    return lax.ppermute(block, axis, [(i, (i + distance) % n) for i in range(n)])


def ring_of(blocks, axis):
    return [shift(block, axis, d + 1) for d, block in enumerate(blocks)]


def shards(projected, weight, beta, gain):
    gain = gain.reshape(1, DK)
    one, state = shaped(DK, 2 * DK), shaped(DK, DK)

    x_far, x_own = fetch_call(projected)
    last = projected[ROWS - (KCONV - 1) :]
    count = lax.axis_size(ALL)
    rim = lax.ppermute(last, ALL, [(i, (i + 1) % count) for i in range(count)])
    mixes_far = mix_call(x_far, weight, True)
    mixes_own = mix_call(x_own, weight, False)
    sent, *far = local_call(mixes_far, weight, rim, beta, True, after=mixes_own[2:])
    came = swap(sent)
    kept_a, *own_a = local_call(mixes_own, weight, rim, beta, False, FIRST)
    chip_a = functools.partial(chip_kernel, which=FIRST)
    across, own = step(chip_a, (kept_a, came), [one, one])
    first, across = across, shift(across, "y", 2)
    kept_b, *own_b = local_call(mixes_own, weight, rim, beta, False, SECOND, (first,))
    chip_b = functools.partial(chip_kernel, which=SECOND)
    after, before = step(chip_b, (kept_b, came), [one, one])

    held = pltpu.VMEM((4, DK, 2 * DK), F32)
    b1, b2, b3 = shift(after, "y", 1), across, shift(before, "y", 3)
    q_far, o_far, far_done = output_call(projected, rim, weight, far, True)
    q_own, o_own, own_done = output_call(projected, rim, weight, own_a + own_b, False, OWN)
    trans, y_prefixes = step(
        y_kernel,
        (own, b2, b1, b3),
        [one, shaped(3, DK, 2 * DK)],
        [held],
        (far_done, own_done),
    )
    b1, b2, b3 = ring_of([trans] * 3, "x")
    trans, x_prefix = step(x_kernel, (trans, b1, b3, b2), [one, one], [held])
    b1, b2, b3 = ring_of([trans] * 3, "z")
    (prefixes,) = step(prefix_kernel, (x_prefix, y_prefixes), [shaped(4, DK, 2 * DK)])

    states = step(
        z_kernel,
        (b1, b3, b2, prefixes),
        [state] * 4,
        [pltpu.VMEM((4, DK, DK), F32)],
    )
    s1, s2, s3 = ring_of(states[1:], "y")
    s_own, goes = step(core_kernel, (kept_a, kept_b, came, states[0], s2, s1, s3), [shaped(HALF, DK, DK)] * 2)
    s_far = swap(goes)
    half = jax.ShapeDtypeStruct((ROWS, HALF * DK), BF16)
    (own,) = step(final_own_kernel, (q_own, o_own, s_own, gain), [half])
    out = jax.ShapeDtypeStruct((ROWS, H * DK), BF16)
    return step(final_kernel, (q_far, o_far, s_far, gain, own), [out])[0]


def solution(mesh):
    grid = Mesh(mesh.devices.reshape(4, 4, 4, 2), ALL)
    placed = (P(ALL, None), P(), P(None, ALL), P())
    return jax.shard_map(
        shards, mesh=grid, in_specs=placed, out_specs=P(ALL, None), check_vma=False
    )
```

```python
import functools

import jax
import jax.numpy as jnp
from jax import lax
from jax.experimental import pallas as pl
from jax.experimental.pallas import tpu as pltpu
from jax.sharding import Mesh
from jax.sharding import PartitionSpec as P

H = 8
DK = 128
KCONV = 4
HALF = H // 2
ROWS = 256
F32, BF16 = jnp.float32, jnp.bfloat16
ALL = ("z", "x", "y", "core")
VMEM_BYTES = 48 * 1024 * 1024
FETCH_BYTES = 52 * 1024 * 1024
FETCH_FLOPS = 10**9


def split(a):
    high = a.astype(BF16)
    return high, (a - high.astype(F32)).astype(BF16)


def dot(a, b):
    return jnp.dot(a, b, preferred_element_type=F32)


def mm(a, b):
    a_high, a_low = split(a)
    b_high, b_low = split(b)
    wide = jnp.concatenate([b_high, b_low], 1)
    r = dot(jnp.concatenate([a_high, a_low], 1), jnp.concatenate([wide, wide], 0))
    n = b.shape[1]
    return r[:, :n] + r[:, n:]


def mmw(a, b):
    a_high, a_low = split(a)
    b_high, b_low = split(b)
    if a.shape[1] == 128:
        r = dot(jnp.concatenate([a_high, a_low], 1), jnp.concatenate([b_high, b_high], 0))
        return r + dot(a_high, b_low)
    return (dot(a_high, b_high) + dot(a_low, b_high)) + dot(a_high, b_low)


def places(size):
    r = lax.broadcasted_iota(jnp.int32, (size, size), 0)
    c = lax.broadcasted_iota(jnp.int32, (size, size), 1)
    return r, c


def alternate(a, size):
    return jnp.concatenate([a[i : i + size] for i in range(size, 128, 2 * size)], 0)


def between(upper, lower, size):
    parts = []
    for i in range(0, 64, size):
        parts += [upper[i : i + size], lower[i : i + size]]
    return jnp.concatenate(parts, 0)


def unit_lower_inverses(inners):
    r, c = places(128)
    lane = lax.broadcasted_iota(jnp.int32, (16, 128), 1)
    row = lax.broadcasted_iota(jnp.int32, (16, 128), 0)
    folded = []
    for a in inners:
        f = jnp.zeros((16, 128), F32)
        for b in range(8):
            f = jnp.where(lane // 16 == b, a[16 * b : 16 * b + 16], f)
        folded.append(f)
    inv = [jnp.where(row == lane % 16, 1.0, 0.0)] * len(inners)
    for j in range(15):
        spread = (lane // 16) * 16 + j
        inv = [
            x
            - jnp.where(
                row > j, jnp.take_along_axis(f, spread, axis=1, mode="promise_in_bounds"), 0.0
            )
            * x[j : j + 1]
            for f, x in zip(folded, inv)
        ]
    inv = [jnp.where(r // 16 == c // 16, jnp.concatenate([x] * 8, 0), 0.0) for x in inv]
    zero = jnp.zeros((64, 128), F32)
    for size in (16, 32, 64):
        below = ((r // (2 * size)) == (c // (2 * size))) & ((r // size) != (c // size))
        part = [mm(alternate(jnp.where(below, a, 0.0), size), d) for a, d in zip(inners, inv)]
        low = [
            alternate(d, size) - mm(alternate(d, size), between(zero, m, size))
            for d, m in zip(inv, part)
        ]
        inv = [
            between(
                jnp.concatenate([d[i : i + size] for i in range(0, 128, 2 * size)], 0), x, size
            )
            for d, x in zip(inv, low)
        ]
    return inv


def unit(values):
    return values * lax.rsqrt(jnp.sum(values * values, -1, keepdims=True) + 1e-06)


def silu(a):
    return a / (1.0 + jnp.exp(-a))


def taps(w, rows, scratch, count):
    acc = w[0:1, :] * scratch[5 : 5 + count, :]
    for j in range(1, KCONV):
        acc = acc + w[j : j + 1, :] * scratch[5 + j : 5 + j + count, :]
    return silu(acc)


def columns(h):
    return slice(h * DK, (h + 1) * DK)


def half_of(at, other):
    return 1 - at[3] if other else at[3]


def head_columns(part, half, h):
    return pl.ds(pl.multiple_of((part * H + half * HALF + h) * DK, DK), DK)


HEADS = range(HALF)
FIRST, SECOND = (2, 0), (1, 3)
OWN = FIRST + SECOND


def fetch_kernel(at, x_all, x_far, x_own, sems):
    copies = []
    for g, to in enumerate((x_far, x_own)):
        for p in range(2):
            begin = ((p + 1) * H + half_of(at, g == 0) * HALF) * DK
            cols = pl.ds(pl.multiple_of(begin, HALF * DK), HALF * DK)
            copies.append(
                pltpu.make_async_copy(x_all.at[:, cols], to.at[p], sems.at[2 * g + p])
            )
    for copy in copies:
        copy.start()
    for copy in copies:
        copy.wait()


def mix_kernel(at, x, w, keys_out, values_out, x_out, scratch, *, other):
    half = half_of(at, other)
    for p in range(2):
        for h in HEADS:
            held = scratch.at[p, h]
            held[0:8, :] = jnp.zeros((8, DK), F32)
            held[8 : 8 + ROWS, :] = x[p, :, columns(h)].astype(F32)
            x_out[p, :, columns(h)] = held[8:16, :]
            m = taps(w[:, head_columns(p + 1, half, h)], ROWS, held, ROWS)
            if p == 0:
                keys_out[h] = unit(m)
            else:
                values_out[h] = m


def at_head(h):
    return pl.ds(pl.multiple_of(h * DK, DK), DK)


def picked(at, which):
    if which is None:
        return list(HEADS)
    return [lax.rem(at[2] + d, 4) for d in which]


def rim_of(at, rim, cols):
    first = at[0] + at[1] + at[2] + at[3] == 0
    return jnp.where(first, 0.0, rim[:, cols].astype(F32))


def first_rows(rim, x, w, scratch):
    scratch[5:8, :] = rim
    scratch[8:16, :] = x
    return taps(w, 8, scratch, 8)


def local_kernel(
    at, keys_in, values_in, x, w, rim, beta, trans_out, keys_out, solved_out, scratch, *, other, which
):
    half = half_of(at, other)
    heads = picked(at, which)
    n = len(heads)

    def with_rim(p, i, h, rest):
        first = first_rows(
            rim_of(at, rim, head_columns(p + 1, half, h)),
            x[p, :, at_head(h)],
            w[:, head_columns(p + 1, half, h)],
            scratch.at[p, i],
        )
        return jnp.concatenate([unit(first) if p == 0 else first, rest[h, 8:, :]], 0)

    keys = [with_rim(0, i, h, keys_in) for i, h in enumerate(heads)]
    values = [with_rim(1, i, h, values_in) for i, h in enumerate(heads)]
    keys_t = [k.T * beta[pl.ds(half * HALF + h, 1), :] for h, k in zip(heads, keys)]
    r, c = places(128)
    strict = r > c
    top = [jnp.where(strict, mm(k[:128], kt[:, :128]), 0.0) for k, kt in zip(keys, keys_t)]
    below = [mmw(k[128:], kt) for k, kt in zip(keys, keys_t)]
    inner = top + [jnp.where(strict, a[:, 128:], 0.0) for a in below]
    right = [jnp.concatenate([k, v], 1) for k, v in zip(keys, values)]
    inv = unit_lower_inverses(inner)
    first = [mmw(d, x[:128]) for d, x in zip(inv[:n], right)]
    rest = [x[128:] - mmw(a[:, :128], y) for x, a, y in zip(right, below, first)]
    second = [mmw(d, z) for d, z in zip(inv[n:], rest)]
    solved = [jnp.concatenate([a, b], 0) for a, b in zip(first, second)]
    trans = [mmw(kt, y) for kt, y in zip(keys_t, solved)]
    for h in range(n):
        trans_out[h, :, :DK] = jnp.where(r == c, 1.0, 0.0) - trans[h][:, :DK]
        trans_out[h, :, DK:] = trans[h][:, DK:]
        keys_out[h] = keys_t[h]
        solved_out[h] = solved[h]


def output_kernel(at, x, rim, w, *refs, other, which):
    blocks, (q_out, o_out, token, scratch) = refs[:-4], refs[-4:]
    token[...] = jnp.zeros_like(token)
    half = half_of(at, other)
    size = HALF * 2 // len(blocks)
    keys_t = [blocks[2 * (i // size)].at[i % size] for i in HEADS]
    solved = [blocks[2 * (i // size) + 1].at[i % size] for i in HEADS]
    queries = []
    for i, h in enumerate(picked(at, which)):
        held, cols = scratch.at[i], head_columns(0, half, h)
        held[5:8, :] = rim_of(at, rim, cols)
        held[8 : 8 + ROWS, :] = x[:, cols].astype(F32)
        queries.append(unit(taps(w[:, cols], ROWS, held, ROWS)))
    r, c = places(ROWS)
    scores = [jnp.where(r >= c, mmw(q, keys_t[h][...]), 0.0) for h, q in zip(HEADS, queries)]
    out = [mmw(s, solved[h][...]) for h, s in zip(HEADS, scores)]
    for h in HEADS:
        q_out[h] = queries[h] - out[h][:, :DK]
        o_out[h] = out[h][:, DK:]


def compose(later, earlier):
    m = mmw(later[:, :DK], earlier)
    return jnp.concatenate([m[:, :DK], m[:, DK:] + later[:, DK:]], 1)


def enter(trans, state):
    return mm(trans[:, :DK], state) + trans[:, DK:]


def ordered(own_first, own, other):
    return jnp.where(own_first, other, own), jnp.where(own_first, own, other)


def chip_kernel(at, kept, came, *outs, which):
    for i, (out, j) in enumerate(zip(outs, picked(at, which))):
        out[...] = compose(*ordered(at[3] == 0, kept[i], came[j]))


def y_kernel(at, b0, b2, b1, b3, total, prefixes, held):
    y = at[2]
    for d, block in enumerate((b0, b1, b2, b3)):
        held[lax.rem(y + 4 - d, 4)] = block[...]
    one = held[0]
    two = compose(held[1], one)
    upper = compose(held[3], held[2])
    prefixes[0] = one
    prefixes[1] = two
    prefixes[2] = compose(held[2], two)
    total[...] = compose(upper, two)


def x_kernel(at, b0, b1, b3, b2, total, prefix, held):
    x = at[1]
    for d, block in enumerate((b0, b1, b2, b3)):
        held[lax.rem(x + 4 - d, 4)] = block[...]
    one = held[0]
    two = compose(held[1], one)
    upper = compose(held[3], held[2])
    three = compose(held[2], two)
    r, c = places(DK)
    none = jnp.concatenate([jnp.where(r == c, 1.0, 0.0), jnp.zeros((DK, DK), F32)], 1)
    prefix[...] = jnp.where(
        x < 2, jnp.where(x == 0, none, one), jnp.where(x == 2, two, three)
    )
    total[...] = compose(upper, two)


def prefix_kernel(at, x_prefix, y_prefixes, out):
    out[0] = x_prefix[...]
    for i in range(3):
        out[i + 1] = compose(y_prefixes[i], x_prefix[...])


def z_kernel(at, b1, b3, b2, prefixes, s0, s1, s2, s3, states):
    y, z = at[2], at[0]
    state = jnp.where(z >= 3, b3[:, DK:], 0.0)
    state = jnp.where(z >= 2, enter(b2[...], state), 0.0)
    state = jnp.where(z >= 1, enter(b1[...], state), 0.0)
    for i in range(4):
        states[i] = enter(prefixes[i], state)
    for d, out in enumerate((s0, s1, s2, s3)):
        out[...] = states[lax.rem(y + d, 4)]


def core_kernel(at, kept_a, kept_b, came, s0, s2, s1, s3, stays, goes):
    y, low = at[2], at[3] == 0
    own = kept_a[1], kept_b[1], kept_a[0], kept_b[0]
    for d, state in enumerate((s0, s1, s2, s3)):
        j = lax.rem(y + 4 - d, 4)
        first = state[...]
        second = enter(jnp.where(low, own[d], came[j]), first)
        stays[j] = jnp.where(low, first, second)
        goes[j] = jnp.where(low, second, first)


def finished(q, o, s, gain, i, h):
    r = mm(q[i], s[h]) + o[i]
    return (r * lax.rsqrt(jnp.mean(r * r, -1, keepdims=True) + 1e-06) * gain[...]).astype(BF16)


def final_own_kernel(at, q, o, s, gain, out):
    for i, h in enumerate(picked(at, OWN)):
        out[:, at_head(h)] = finished(q, o, s, gain, i, h)


def final_kernel(at, q, o, s, gain, own, out):
    for h in HEADS:
        out[:, head_columns(0, at[3], h)] = own[:, columns(h)]
        out[:, head_columns(0, 1 - at[3], h)] = finished(q, o, s, gain, h, h)


class Place:
    def __getitem__(self, i):
        return lax.axis_index(ALL[i])


def step(kernel, args, outs, scratch=(), after=(), vmem=VMEM_BYTES, hbm=(), flops=10**6):
    args, after, hbm = list(args), list(after), list(hbm)

    def body(*refs):
        kernel(Place(), *refs[: len(args) + len(hbm)], *refs[len(args) + len(hbm) + len(after) :])

    anywhere = pl.BlockSpec(memory_space=pl.ANY)
    return pl.pallas_call(
        body,
        in_specs=[pl.BlockSpec()] * len(args) + [anywhere] * (len(hbm) + len(after)),
        out_shape=list(outs),
        scratch_shapes=list(scratch),
        cost_estimate=pl.CostEstimate(flops=flops, bytes_accessed=2**10, transcendentals=0),
        compiler_params=pltpu.CompilerParams(vmem_limit_bytes=vmem),
    )(*args, *hbm, *after)


def shaped(*shape):
    return jax.ShapeDtypeStruct(shape, F32)


def fetch_call(projected):
    x = jax.ShapeDtypeStruct((2, ROWS, HALF * DK), BF16)
    return step(
        fetch_kernel,
        (),
        [x, x],
        [pltpu.SemaphoreType.DMA((4,))],
        vmem=FETCH_BYTES,
        hbm=(projected,),
        flops=FETCH_FLOPS,
    )


def mix_call(x, weight, other):
    return step(
        functools.partial(mix_kernel, other=other),
        (x, weight),
        [shaped(HALF, ROWS, DK)] * 2 + [shaped(2, 8, HALF * DK)],
        [pltpu.VMEM((2, HALF, ROWS + 8, DK), F32)],
    )


def local_call(mixes, weight, rim, beta, other, which=None, after=()):
    n = HALF if which is None else len(which)
    outs = [shaped(n, DK, 2 * DK), shaped(n, DK, ROWS), shaped(n, ROWS, 2 * DK)]
    return step(
        functools.partial(local_kernel, other=other, which=which),
        (*mixes, weight, rim, beta),
        outs,
        [pltpu.VMEM((2, n, 16, DK), F32)],
        after,
    )


def output_call(projected, rim, weight, blocks, other, which=None):
    outs = [shaped(HALF, ROWS, DK), shaped(HALF, ROWS, DK), shaped(8, DK)]
    return step(
        functools.partial(output_kernel, other=other, which=which),
        (projected, rim, weight, *blocks),
        outs,
        [pltpu.VMEM((HALF, ROWS + 8, DK), F32)],
    )


def swap(block):
    return lax.ppermute(block, "core", [(0, 1), (1, 0)])


def shift(block, axis, distance):
    n = lax.axis_size(axis)
    return lax.ppermute(block, axis, [(i, (i + distance) % n) for i in range(n)])


def ring_of(blocks, axis):
    return [shift(block, axis, d + 1) for d, block in enumerate(blocks)]


def shards(projected, weight, beta, gain):
    gain = gain.reshape(1, DK)
    one, state = shaped(DK, 2 * DK), shaped(DK, DK)

    x_far, x_own = fetch_call(projected)
    last = projected[ROWS - (KCONV - 1) :]
    count = lax.axis_size(ALL)
    rim = lax.ppermute(last, ALL, [(i, (i + 1) % count) for i in range(count)])
    mixes_far = mix_call(x_far, weight, True)
    mixes_own = mix_call(x_own, weight, False)
    sent, *far = local_call(mixes_far, weight, rim, beta, True, after=mixes_own[2:])
    came = swap(sent)
    kept_a, *own_a = local_call(mixes_own, weight, rim, beta, False, FIRST)
    chip_a = functools.partial(chip_kernel, which=FIRST)
    across, own = step(chip_a, (kept_a, came), [one, one])
    first, across = across, shift(across, "y", 2)
    kept_b, *own_b = local_call(mixes_own, weight, rim, beta, False, SECOND, (first,))
    chip_b = functools.partial(chip_kernel, which=SECOND)
    after, before = step(chip_b, (kept_b, came), [one, one])

    held = pltpu.VMEM((4, DK, 2 * DK), F32)
    b1, b2, b3 = shift(after, "y", 1), across, shift(before, "y", 3)
    q_far, o_far, far_done = output_call(projected, rim, weight, far, True)
    q_own, o_own, own_done = output_call(projected, rim, weight, own_a + own_b, False, OWN)
    trans, y_prefixes = step(
        y_kernel,
        (own, b2, b1, b3),
        [one, shaped(3, DK, 2 * DK)],
        [held],
        (far_done,),
    )
    b1, b2, b3 = ring_of([trans] * 3, "x")
    trans, x_prefix = step(x_kernel, (trans, b1, b3, b2), [one, one], [held], (own_done,))
    b1, b2, b3 = ring_of([trans] * 3, "z")
    (prefixes,) = step(prefix_kernel, (x_prefix, y_prefixes), [shaped(4, DK, 2 * DK)])

    states = step(
        z_kernel,
        (b1, b3, b2, prefixes),
        [state] * 4,
        [pltpu.VMEM((4, DK, DK), F32)],
    )
    s1, s2, s3 = ring_of(states[1:], "y")
    s_own, goes = step(core_kernel, (kept_a, kept_b, came, states[0], s2, s1, s3), [shaped(HALF, DK, DK)] * 2)
    s_far = swap(goes)
    half = jax.ShapeDtypeStruct((ROWS, HALF * DK), BF16)
    (own,) = step(final_own_kernel, (q_own, o_own, s_own, gain), [half])
    out = jax.ShapeDtypeStruct((ROWS, H * DK), BF16)
    return step(final_kernel, (q_far, o_far, s_far, gain, own), [out])[0]


def solution(mesh):
    grid = Mesh(mesh.devices.reshape(4, 4, 4, 2), ALL)
    placed = (P(ALL, None), P(), P(None, ALL), P())
    return jax.shard_map(
        shards, mesh=grid, in_specs=placed, out_specs=P(ALL, None), check_vma=False
    )
```
